32 devices in a mesh: row: 8 (over z, core), col: 4 (over y, x).
Axes of the slice: x: 2, y: 2, z: 4, core: 2. Of those that a mesh axis runs over, the one named last changes fastest.
Arguments:
- features: bfloat16 [32768, 64], P(('col', 'row')), may hold values from -6 to 6
- weight: bfloat16 [64, 256], replicated, may hold values from -0.75 to 0.75
- cotangent: bfloat16 [32768, 256], P(('row', 'col')), may hold values from -6 to 6
- tile_values: bfloat16 [8, 4, 384, 128, 128], P('row', 'col'), may hold values from -0.25 to 0.25
- tile_rows: int32 [8, 4, 384], P('row', 'col'), may hold values from 0 to 31
- tile_cols: int32 [8, 4, 384], P('row', 'col'), may hold values from 0 to 63
- tile_counts: int32 [8, 4], P('row', 'col'), may hold values from 1 to 384, as said below
Outputs:
- activations: bfloat16 [32768, 256], P(('row', 'col'))
- feature_grad: bfloat16 [32768, 64], P(('col', 'row'))
- weight_grad: float32 [64, 256], replicated
The draws below stay inside these ranges and needn't reach their ends.
Inputs may be any that keep to these rules, and one draw needn't show every extreme that they name: `tile_counts`: each grid block's number of live tile slots; some grid block uses all 384 slots.
All inputs are finite; a program needn't handle non-finite values.
Results may differ from the reference program's by a relative error of at most 0.006.
Values may be sent and summed in bfloat16 or wider, within the bound.
A program may use at most 128 MiB of HBM per device.

```python
import jax
import jax.numpy as jnp
from jax import lax

TILE = 128
F = 64
HID = 256
ND = 1024
TILES_DEV = 384
NODES = 32768
N_ROW = 8
N_COL = 4


def draw_tile_counts(key, part):
    key = jax.random.fold_in(key, 5)
    levels = jax.random.randint(key, (N_ROW * N_COL,), 1, 17)
    counts = jnp.maximum(1, levels * levels * TILES_DEV // 256)
    chosen = jax.random.randint(jax.random.fold_in(key, 1), (), 0, N_ROW * N_COL)
    counts = jnp.where(jnp.arange(N_ROW * N_COL) == chosen, TILES_DEV, counts)
    return counts.reshape(N_ROW, N_COL).astype(jnp.int32)


def set_ends(values, own_key, least, top_value):
    longest = values.shape.index(max(values.shape))
    spots = []
    for shift in (0, 1):
        where = [jax.random.randint(jax.random.fold_in(own_key, axis), (), 0, length) for axis, length in enumerate(values.shape)]
        where[longest] = (where[longest] + shift) % values.shape[longest]
        spots.append(tuple(where))
    return values.at[spots[0]].set(least).at[spots[1]].set(top_value)


def block_levels(rng, shape, cuts, smallest, high):
    def one(dim, shards_of):
        heights = jax.random.uniform(jax.random.fold_in(jax.random.fold_in(rng, 6), dim), (shards_of,), jnp.float32, smallest / len(cuts), high / len(cuts))
        return jnp.repeat(jnp.exp(heights), shape[dim] // shards_of).reshape((-1,) + (1,) * (len(shape) - dim - 1))

    level = one(*cuts[0])
    for cut in cuts[1:]:
        level = level * one(*cut)
    return level


def bell_draw(key, extent, scale, bound, cuts=(), kind=jnp.bfloat16):
    entries = scale * jax.random.normal(key, extent, jnp.float32)
    if cuts:
        entries = entries * block_levels(key, extent, cuts, -0.22, 0.18)
    return jnp.clip(entries, -bound, bound).astype(kind)


def setup_inputs(seed: int = 0) -> dict:
    streams_of = jax.random.split(jax.random.key(seed), 8)
    return {
        "features": bell_draw(streams_of[0], (NODES, F), 1.0, 6.0, ((0, 32),)),
        "weight": bell_draw(streams_of[1], (F, HID), F ** -0.5, 0.75),
        "cotangent": bell_draw(streams_of[2], (NODES, HID), 1.0, 6.0, ((0, 32),)),
        "tile_values": bell_draw(streams_of[3], (N_ROW, N_COL, TILES_DEV, TILE, TILE), (1.3 * (ND / TILES_DEV) ** 0.5 / TILE), 0.25, ((0, 8), (1, 4))),
        "tile_rows": set_ends(jax.random.randint(streams_of[4], (N_ROW, N_COL, TILES_DEV), 0, ND * N_COL // TILE), jax.random.fold_in(streams_of[4], 1), 0, (ND * N_COL // TILE) - 1).astype(jnp.int32),
        "tile_cols": set_ends(jax.random.randint(streams_of[5], (N_ROW, N_COL, TILES_DEV), 0, ND * N_ROW // TILE), jax.random.fold_in(streams_of[5], 1), 0, (ND * N_ROW // TILE) - 1).astype(jnp.int32),
        "tile_counts": draw_tile_counts(jax.random.fold_in(streams_of[7], 71), 0),
    }


def spread(source, targets, picks, values, inside, out_tiles, transpose):
    tiled = source.reshape(-1, TILE, F)

    def visit(totals, item):
        block_values, target, pick, keep = item
        picked = tiled[pick].astype(jnp.float32)
        matrices = block_values.astype(jnp.float32)
        if transpose:
            product = jnp.einsum("tji,tjf->tif", matrices, picked)
        else:
            product = jnp.einsum("tij,tjf->tif", matrices, picked)
        product = jnp.where(keep[:, None, None], product, 0.0)
        return totals.at[target].add(product), None

    start = jnp.zeros((out_tiles, TILE, F), jnp.float32)
    totals, unused = lax.scan(visit, start, (values, targets, picks, inside))
    return totals.reshape(-1, F)


def reference(features, weight, cotangent, tile_values, tile_rows, tile_cols, tile_counts):
    grid = N_ROW * N_COL
    out_tiles = ND * N_ROW * N_COL // TILE
    values = tile_values.reshape(grid, TILES_DEV, TILE, TILE)
    rows = tile_rows.reshape(grid, TILES_DEV).astype(jnp.int32)
    cols = tile_cols.reshape(grid, TILES_DEV).astype(jnp.int32)
    counts = tile_counts.reshape(grid).astype(jnp.int32)
    device = jnp.arange(grid, dtype=jnp.int32)
    row_block = device // N_COL
    col_block = device % N_COL
    global_rows = row_block[:, None] * (ND * N_COL // TILE) + rows
    global_cols = col_block[:, None] * (ND * N_ROW // TILE) + cols
    inside = jnp.arange(TILES_DEV, dtype=jnp.int32)[None, :] < counts[:, None]
    aggregated = spread(features, global_rows, global_cols, values, inside, out_tiles, False)
    aggregated_low = aggregated.astype(jnp.bfloat16)
    pre = jnp.dot(aggregated_low, weight, preferred_element_type=jnp.float32)
    activations = jax.nn.silu(pre).astype(jnp.bfloat16)
    sigma = jax.nn.sigmoid(pre)
    pre_grad = (cotangent.astype(jnp.float32) * sigma * (1.0 + pre * (1.0 - sigma))).astype(jnp.bfloat16)
    aggregated_grad = jnp.dot(pre_grad, weight.T, preferred_element_type=jnp.float32).astype(jnp.bfloat16)
    feature_grad = spread(aggregated_grad, global_cols, global_rows, values, inside, out_tiles, True).astype(jnp.bfloat16)
    weight_grad = jnp.dot(aggregated_low.T, pre_grad, preferred_element_type=jnp.float32)
    return activations, feature_grad, weight_grad
```

```python
import functools

import jax
import jax.numpy as jnp
from jax import lax
from jax.experimental import pallas as pl
from jax.experimental.pallas import tpu as pltpu
from jax.sharding import PartitionSpec as P

MESH = pl.DeviceIdType.MESH
F32 = jnp.float32
BF16 = jnp.bfloat16
VMEM_LIMIT = 40 * 1024 * 1024


def dot(a, b, contract_a, contract_b):
    return lax.dot_general(
        a, b, (((contract_a,), (contract_b,)), ((), ())), preferred_element_type=F32
    )


def greet(peers):
    barrier = pltpu.get_barrier_semaphore()
    for peer in peers:
        pl.semaphore_signal(barrier, inc=1, device_id=peer, device_id_type=MESH)
    return lambda: pl.semaphore_wait(barrier, len(peers))


def remote(src, dst, send_sem, recv_sem, peer):
    return pltpu.make_async_remote_copy(
        src_ref=src,
        dst_ref=dst,
        send_sem=send_sem,
        recv_sem=recv_sem,
        device_id=peer,
        device_id_type=MESH,
    )


def gather_kernel(n_row, f_ref, out_ref, own, local_sem, send_sem, recv_sem):
    chips = n_row // 2
    me = lax.axis_index("row")
    chip, core = me // 2, me % 2
    partner = {"row": chip * 2 + 1 - core}
    lane = [{"row": lax.rem(chip + d, chips) * 2 + core} for d in range(1, chips)]
    ready = greet(lane + [partner])
    tiles = own.shape[0]
    for t in range(tiles):
        own[t] = f_ref[t * 128 : (t + 1) * 128, :].astype(F32).T.astype(BF16)
    keep = pltpu.make_async_copy(own, out_ref.at[me], local_sem)
    keep.start()
    ready()
    copies = []
    for d in range(1, chips):
        copies.append(remote(own, out_ref.at[me], send_sem.at[d - 1], recv_sem.at[d - 1], lane[d - 1]))
    copies.append(remote(own, out_ref.at[me], send_sem.at[chips - 1], recv_sem.at[chips - 1], partner))
    for copy in copies:
        copy.start()
    for d in range(1, chips):
        came = lax.rem(chip + chips - d, chips) * 2 + core
        remote(own, out_ref.at[came], send_sem.at[d - 1], recv_sem.at[d - 1], partner).wait_recv()
        k = chips - 1 + d
        copy = remote(out_ref.at[came], out_ref.at[came], send_sem.at[k], recv_sem.at[k], partner)
        copy.start()
        copies.append(copy)
    for d in range(chips):
        came = lax.rem(chip + chips - d, chips) * 2 + 1 - core
        k = chips - 1 + d
        remote(own, out_ref.at[came], send_sem.at[k], recv_sem.at[k], partner).wait_recv()
    for copy in copies:
        copy.wait_send()
    keep.wait()


def gather_features(features, n_row):
    rows, width = features.shape
    tiles = rows // 128
    chips = n_row // 2
    return pl.pallas_call(
        functools.partial(gather_kernel, n_row),
        out_shape=jax.ShapeDtypeStruct((n_row, tiles, width, 128), BF16),
        in_specs=[pl.BlockSpec(memory_space=pltpu.VMEM)],
        out_specs=pl.BlockSpec(memory_space=pl.ANY),
        scratch_shapes=[
            pltpu.VMEM((tiles, width, 128), BF16),
            pltpu.SemaphoreType.DMA,
            pltpu.SemaphoreType.DMA((2 * chips - 1,)),
            pltpu.SemaphoreType.DMA((2 * chips - 1,)),
        ],
        compiler_params=pltpu.CompilerParams(
            collective_id=0, has_side_effects=True, vmem_limit_bytes=VMEM_LIMIT
        ),
        name="gather_features",
    )(features)


def tile_kernel(
    transpose, group, live_ref, targets_ref, picks_ref, values_ref, source_ref, out_ref, acc
):
    step = pl.program_id(0)
    per_step = values_ref.shape[0]
    n_targets = out_ref.shape[0]
    live = live_ref[0]

    @pl.when(step == 0)
    def _():
        acc[...] = jnp.zeros_like(acc)

    def body(g, carry):
        for u in range(group):
            local = g * group + u
            slot = step * per_step + local
            pick = picks_ref[slot]
            target = jnp.where(slot < live, targets_ref[slot], n_targets)
            product = dot(source_ref[pick], values_ref[local], 1, 0 if transpose else 1)
            acc[target] += product
        return carry

    left = live - step * per_step
    groups = jnp.clip((left + group - 1) // group, 0, per_step // group)
    lax.fori_loop(0, groups, body, 0)

    @pl.when(step == pl.num_programs(0) - 1)
    def _():
        out_ref[...] = acc[0:n_targets].astype(BF16)


def tile_pass(values, targets, picks, live, source, n_targets, transpose):
    slots, side, _ = values.shape
    n_sources, width, _ = source.shape
    per_step, group = 48, 16
    whole = pl.BlockSpec(memory_space=pltpu.SMEM)
    return pl.pallas_call(
        functools.partial(tile_kernel, transpose, group),
        out_shape=jax.ShapeDtypeStruct((n_targets, width, side), BF16),
        grid=(slots // per_step,),
        in_specs=[
            whole,
            whole,
            whole,
            pl.BlockSpec((per_step, side, side), lambda i: (i, 0, 0)),
            pl.BlockSpec((n_sources, width, side), lambda i: (0, 0, 0)),
        ],
        out_specs=pl.BlockSpec((n_targets, width, side), lambda i: (0, 0, 0)),
        scratch_shapes=[pltpu.VMEM((n_targets + 1, width, side), F32)],
        compiler_params=pltpu.CompilerParams(vmem_limit_bytes=VMEM_LIMIT),
        cost_estimate=pl.CostEstimate(
            flops=2 * slots * side * side * width,
            bytes_accessed=2 * slots * side * side,
            transcendentals=0,
        ),
        name="tiles_backward" if transpose else "tiles_forward",
    )(live, targets, picks, values, source)


def node_kernel(
    n_row, n_col,
    part_ref, weight_ref, cot_ref,
    act_ref, grads_ref, chunk_ref,
    came, own_grad, wgrad, wcame,
    local_sem, a_send, a_recv, g_send, g_recv, w_send, w_recv,
):
    row, col = lax.axis_index("row"), lax.axis_index("col")
    across = [{"col": lax.rem(col + d, n_col)} for d in range(1, n_col)]
    along = [lax.rem(row + d, n_row) for d in range(1, n_row)]
    ready = greet(across + [{"row": r} for r in along])
    ready()
    copies = []
    for d in range(1, n_col):
        target = lax.rem(col + d, n_col)
        copies.append(remote(part_ref.at[target], came.at[d - 1], a_send.at[d - 1], a_recv.at[d - 1], across[d - 1]))
    for copy in copies:
        copy.start()
    for copy in copies:
        copy.wait_recv()
    tiles = own_grad.shape[0]
    weight = weight_ref[...]
    total = None
    for t in range(tiles):
        agg = part_ref[col, t].astype(F32)
        for d in range(1, n_col):
            agg += came[d - 1, t].astype(F32)
        low = agg.astype(BF16)
        nodes = slice(t * 128, (t + 1) * 128)
        pre = jnp.dot(agg.T.astype(BF16), weight, preferred_element_type=F32)
        sigma = 1.0 / (1.0 + jnp.exp(-pre))
        act_ref[nodes, :] = (pre * sigma).astype(BF16)
        cot = cot_ref[nodes, :].astype(F32)
        pre_grad = (cot * sigma * (1.0 + pre * (1.0 - sigma))).astype(BF16)
        own_grad[t] = dot(weight, pre_grad, 1, 1).astype(BF16)
        term = jnp.dot(low, pre_grad, preferred_element_type=F32)
        total = term if total is None else total + term
    keep = pltpu.make_async_copy(own_grad, grads_ref.at[col], local_sem)
    keep.start()
    for d in range(1, n_col):
        copy = remote(own_grad, grads_ref.at[col], g_send.at[d - 1], g_recv.at[d - 1], across[d - 1])
        copy.start()
        copies.append(copy)
    depth = wgrad.shape[1]
    for r in range(n_row):
        wgrad[r] = total[r * depth : (r + 1) * depth]
    w_copies = []
    for d in range(1, n_row):
        r = along[d - 1]
        copy = remote(wgrad.at[r], wcame.at[d - 1], w_send.at[d - 1], w_recv.at[d - 1], {"row": r})
        copy.start()
        w_copies.append(copy)
    for copy in w_copies:
        copy.wait_recv()
    chunk = wgrad[row]
    for d in range(1, n_row):
        chunk += wcame[d - 1]
    chunk_ref[...] = chunk
    for d in range(1, n_col):
        source = lax.rem(col + n_col - d, n_col)
        remote(own_grad, grads_ref.at[source], g_send.at[d - 1], g_recv.at[d - 1], across[d - 1]).wait_recv()
    for copy in copies + w_copies:
        copy.wait_send()
    keep.wait()


def node_step(part, weight, cotangent, n_row, n_col):
    _, tiles, width, side = part.shape
    hidden = weight.shape[1]
    depth = width // n_row
    vmem = pl.BlockSpec(memory_space=pltpu.VMEM)
    dma = pltpu.SemaphoreType.DMA
    return pl.pallas_call(
        functools.partial(node_kernel, n_row, n_col),
        out_shape=(
            jax.ShapeDtypeStruct(cotangent.shape, BF16),
            jax.ShapeDtypeStruct(part.shape, BF16),
            jax.ShapeDtypeStruct((depth, hidden), F32),
        ),
        in_specs=[vmem, vmem, vmem],
        out_specs=(vmem, pl.BlockSpec(memory_space=pl.ANY), vmem),
        scratch_shapes=[
            pltpu.VMEM((n_col - 1, tiles, width, side), BF16),
            pltpu.VMEM((tiles, width, side), BF16),
            pltpu.VMEM((n_row, depth, hidden), F32),
            pltpu.VMEM((n_row - 1, depth, hidden), F32),
            dma,
            dma((n_col - 1,)),
            dma((n_col - 1,)),
            dma((n_col - 1,)),
            dma((n_col - 1,)),
            dma((n_row - 1,)),
            dma((n_row - 1,)),
        ],
        compiler_params=pltpu.CompilerParams(
            collective_id=1, has_side_effects=True, vmem_limit_bytes=VMEM_LIMIT
        ),
        name="node_step",
    )(part, weight, cotangent)


def scatter_kernel(
    n_row, n_col,
    part_ref, chunk_ref,
    out_ref, wgrad_ref,
    other, chip_sum, came, wcols, wsum,
    p_send, p_recv, l_send, l_recv, c_send, c_recv, w_send, w_recv,
):
    chips = n_row // 2
    row, col = lax.axis_index("row"), lax.axis_index("col")
    chip, core = row // 2, row % 2
    partner = {"row": chip * 2 + 1 - core}
    along = [lax.rem(row + d, n_row) for d in range(1, n_row)]
    across = [{"col": lax.rem(col + d, n_col)} for d in range(1, n_col)]
    ready = greet([{"row": r} for r in along] + across)
    ready()
    copies = []
    order = list(range(1, chips)) + [0]
    pairs = []
    for d in order:
        k = lax.rem(chip + d, chips)
        copy = remote(part_ref.at[k * 2 + 1 - core], other.at[d], p_send.at[d], p_recv.at[d], partner)
        copy.start()
        pairs.append(copy)
    for d in range(1, n_col):
        copy = remote(chunk_ref, wcols.at[col], c_send.at[d - 1], c_recv.at[d - 1], across[d - 1])
        copy.start()
        copies.append(copy)
    wcols[col] = chunk_ref[...]
    lanes = []
    for i, d in enumerate(order):
        pairs[i].wait_recv()
        if d == 0:
            continue
        k = lax.rem(chip + d, chips)
        chip_sum[d - 1] = (part_ref[k * 2 + core].astype(F32) + other[d].astype(F32)).astype(BF16)
        copy = remote(chip_sum.at[d - 1], came.at[d - 1], l_send.at[d - 1], l_recv.at[d - 1], {"row": k * 2 + core})
        copy.start()
        lanes.append(copy)
    for d in range(1, n_col):
        source = lax.rem(col + n_col - d, n_col)
        remote(chunk_ref, wcols.at[source], c_send.at[d - 1], c_recv.at[d - 1], across[d - 1]).wait_recv()
    total = wcols[0]
    for c in range(1, n_col):
        total += wcols[c]
    wsum[...] = total
    wgrad_ref[row] = total
    for d in range(1, n_row):
        copy = remote(wsum, wgrad_ref.at[row], w_send.at[d - 1], w_recv.at[d - 1], {"row": along[d - 1]})
        copy.start()
        copies.append(copy)
    for copy in lanes:
        copy.wait_recv()
    for t in range(out_ref.shape[0]):
        block = part_ref[row, t].astype(F32) + other[0, t].astype(F32)
        for d in range(1, chips):
            block += came[d - 1, t].astype(F32)
        out_ref[t] = block.astype(BF16)
    for d in range(1, n_row):
        source = lax.rem(row + n_row - d, n_row)
        remote(wsum, wgrad_ref.at[source], w_send.at[d - 1], w_recv.at[d - 1], partner).wait_recv()
    for copy in copies + pairs + lanes:
        copy.wait_send()


def scatter_step(part, chunk, n_row, n_col):
    _, tiles, width, side = part.shape
    depth, hidden = chunk.shape
    chips = n_row // 2
    vmem = pl.BlockSpec(memory_space=pltpu.VMEM)
    dma = pltpu.SemaphoreType.DMA
    return pl.pallas_call(
        functools.partial(scatter_kernel, n_row, n_col),
        out_shape=(
            jax.ShapeDtypeStruct((tiles, width, side), BF16),
            jax.ShapeDtypeStruct((n_row, depth, hidden), F32),
        ),
        in_specs=[vmem, vmem],
        out_specs=(vmem, vmem),
        scratch_shapes=[
            pltpu.VMEM((chips, tiles, width, side), BF16),
            pltpu.VMEM((chips - 1, tiles, width, side), BF16),
            pltpu.VMEM((chips - 1, tiles, width, side), BF16),
            pltpu.VMEM((n_col, depth, hidden), F32),
            pltpu.VMEM((depth, hidden), F32),
            dma((chips,)),
            dma((chips,)),
            dma((chips - 1,)),
            dma((chips - 1,)),
            dma((n_col - 1,)),
            dma((n_col - 1,)),
            dma((n_row - 1,)),
            dma((n_row - 1,)),
        ],
        compiler_params=pltpu.CompilerParams(
            collective_id=2, has_side_effects=True, vmem_limit_bytes=VMEM_LIMIT
        ),
        name="scatter_step",
    )(part, chunk)


def on_device(n_row, n_col, features, weight, cotangent, tile_values, tile_rows, tile_cols, tile_counts):
    own_rows, width = features.shape
    tiles = own_rows // 128
    values = tile_values[0, 0]
    rows = tile_rows[0, 0]
    cols = tile_cols[0, 0]
    live = tile_counts[0]
    sources = gather_features(features, n_row).reshape(n_row * tiles, width, 128)
    part = tile_pass(values, rows, cols, live, sources, n_col * tiles, False)
    activations, grads, chunk = node_step(
        part.reshape(n_col, tiles, width, 128), weight, cotangent, n_row, n_col
    )
    grads = grads.reshape(n_col * tiles, width, 128)
    grad_part = tile_pass(values, cols, rows, live, grads, n_row * tiles, True)
    out, weight_grad = scatter_step(
        grad_part.reshape(n_row, tiles, width, 128), chunk, n_row, n_col
    )
    feature_grad = jnp.swapaxes(out, 1, 2).reshape(own_rows, width)
    return activations, feature_grad, weight_grad.reshape(weight.shape)


def solution(mesh):
    in_specs = (
        P(("col", "row"), None),
        P(),
        P(("row", "col"), None),
        P("row", "col", None, None, None),
        P("row", "col", None),
        P("row", "col", None),
        P("row", "col"),
    )
    out_specs = (P(("row", "col"), None), P(("col", "row"), None), P())
    return jax.shard_map(
        functools.partial(on_device, mesh.shape["row"], mesh.shape["col"]),
        mesh=mesh,
        in_specs=in_specs,
        out_specs=out_specs,
        check_vma=False,
    )
```

```python
import functools

import jax
import jax.numpy as jnp
from jax import lax
from jax.experimental import pallas as pl
from jax.experimental.pallas import tpu as pltpu
from jax.sharding import PartitionSpec as P

MESH = pl.DeviceIdType.MESH
F32 = jnp.float32
BF16 = jnp.bfloat16
VMEM_LIMIT = 24 * 1024 * 1024
GATHER_VMEM_LIMIT = 39 * 1024 * 1024
PIECES = 2
GROUP = 16


def inside(chip, chips):
    return (chip >= 0) & (chip < chips)


def dot(a, b, contract_a, contract_b):
    return lax.dot_general(
        a, b, (((contract_a,), (contract_b,)), ((), ())), preferred_element_type=F32
    )


def greet(peers):
    barrier = pltpu.get_barrier_semaphore()
    for peer in peers:
        pl.semaphore_signal(barrier, inc=1, device_id=peer, device_id_type=MESH)
    return lambda: pl.semaphore_wait(barrier, len(peers))


def greet_line(chip, core, chips, peers):
    barrier = pltpu.get_barrier_semaphore()
    for peer in peers:
        pl.semaphore_signal(barrier, inc=1, device_id=peer, device_id_type=MESH)
    count = len(peers)
    for sign in (1, -1):
        there = inside(chip + sign, chips)
        count += there.astype(jnp.int32)

        @pl.when(there)
        def _():
            pl.semaphore_signal(
                barrier, inc=1, device_id={"row": (chip + sign) * 2 + core}, device_id_type=MESH
            )

    return lambda: pl.semaphore_wait(barrier, count)


def remote(src, dst, send_sem, recv_sem, peer):
    return pltpu.make_async_remote_copy(
        src_ref=src,
        dst_ref=dst,
        send_sem=send_sem,
        recv_sem=recv_sem,
        device_id=peer,
        device_id_type=MESH,
    )


def gather_kernel(n_row, f_ref, values_ref, out_ref, kept_ref, load_sem, l_send, l_recv, p_send, p_recv):
    chips = n_row // 2
    me = lax.axis_index("row")
    chip, core = me // 2, me % 2
    partner = {"row": chip * 2 + 1 - core}
    tiles = out_ref.shape[1]
    half = tiles // PIECES
    load = pltpu.make_async_copy(values_ref, kept_ref, load_sem)
    load.start()
    ready = greet_line(chip, core, chips, [partner])
    for t in range(tiles):
        out_ref[me, t] = f_ref[:, t * 128 : (t + 1) * 128]
    ready()

    def block(source, q):
        return out_ref.at[source, pl.ds(q * half, half)]

    def lane(side, hop, q, source, sign):
        piece = block(source, q)
        return remote(
            piece, piece, l_send.at[side, hop - 1, q], l_recv.at[side, hop - 1, q],
            {"row": me + 2 * sign},
        )

    def across(side, hop, q, source):
        piece = block(source, q)
        return remote(piece, piece, p_send.at[side, hop, q], p_recv.at[side, hop, q], partner)

    sides = ((0, 1), (1, -1))
    for q in range(PIECES):
        for side, sign in sides:
            @pl.when(inside(chip + sign, chips))
            def _():
                lane(side, 1, q, me, sign).start()
        across(0, 0, q, me).start()
    for hop in range(1, chips):
        for q in range(PIECES):
            for side, sign in sides:
                source = me - 2 * sign * hop
                came = inside(chip - sign * hop, chips)

                @pl.when(came)
                def _():
                    lane(side, hop, q, source, sign).wait_recv()

                if hop + 1 < chips:
                    @pl.when(came & inside(chip + sign, chips))
                    def _():
                        lane(side, hop + 1, q, source, sign).start()

                @pl.when(came)
                def _():
                    across(side, hop, q, source).start()
    for q in range(PIECES):
        across(0, 0, q, chip * 2 + 1 - core).wait_recv()
        across(0, 0, q, me).wait_send()
        for side, sign in sides:
            @pl.when(inside(chip + sign, chips))
            def _():
                lane(side, 1, q, me, sign).wait_send()
    for hop in range(1, chips):
        for q in range(PIECES):
            for side, sign in sides:
                source = me - 2 * sign * hop
                came = inside(chip - sign * hop, chips)

                @pl.when(came)
                def _():
                    across(side, hop, q, (chip - sign * hop) * 2 + 1 - core).wait_recv()
                    across(side, hop, q, source).wait_send()

                if hop + 1 < chips:
                    @pl.when(came & inside(chip + sign, chips))
                    def _():
                        lane(side, hop + 1, q, source, sign).wait_send()
    load.wait()


def gather_features(features, values, n_row):
    width, rows = features.shape
    tiles = rows // 128
    chips = n_row // 2
    vmem = pl.BlockSpec(memory_space=pltpu.VMEM)
    dma = pltpu.SemaphoreType.DMA
    return pl.pallas_call(
        functools.partial(gather_kernel, n_row),
        out_shape=(
            jax.ShapeDtypeStruct((n_row, tiles, width, 128), BF16),
            jax.ShapeDtypeStruct(values.shape, BF16),
        ),
        in_specs=[vmem, pl.BlockSpec(memory_space=pl.ANY)],
        out_specs=(vmem, vmem),
        scratch_shapes=[
            dma,
            dma((2, chips - 1, PIECES)),
            dma((2, chips - 1, PIECES)),
            dma((2, chips, PIECES)),
            dma((2, chips, PIECES)),
        ],
        compiler_params=pltpu.CompilerParams(
            collective_id=0, has_side_effects=True, vmem_limit_bytes=GATHER_VMEM_LIMIT
        ),
        name="gather_features",
    )(features, values)


def add_tiles(transpose, live_ref, targets_ref, picks_ref, values_ref, source_ref, acc):
    group = GROUP
    live = live_ref[0, 0]
    spare = acc.shape[0] - 1
    acc[...] = jnp.zeros_like(acc)

    def body(g, carry):
        for u in range(group):
            slot = g * group + u
            pick = picks_ref[0, 0, slot]
            target = jnp.where(slot < live, targets_ref[0, 0, slot], spare)
            product = dot(source_ref[pick], values_ref[slot], 1, 0 if transpose else 1)
            acc[target] += product
        return carry

    groups = (live + group - 1) // group
    lax.fori_loop(0, groups, body, 0)


def forward_kernel(live_ref, rows_ref, cols_ref, values_ref, source_ref, out_ref, acc):
    add_tiles(False, live_ref, rows_ref, cols_ref, values_ref, source_ref, acc)
    out_ref[...] = acc[0 : out_ref.shape[0]].astype(BF16)


def backward_kernel(
    live_ref, rows_ref, cols_ref, values_ref, source_ref, act_ref, out_ref, act_out_ref, sem
):
    write = pltpu.make_async_copy(act_ref, act_out_ref, sem)
    write.start()
    add_tiles(True, live_ref, cols_ref, rows_ref, values_ref, source_ref, out_ref)
    write.wait()


def tile_pass(values, rows, cols, live, source, n_targets, activations=None):
    slots, side, _ = values.shape
    width = source.shape[1]
    smem = pl.BlockSpec(memory_space=pltpu.SMEM)
    vmem = pl.BlockSpec(memory_space=pltpu.VMEM)
    cost = pl.CostEstimate(
        flops=2 * slots * side * side * width,
        bytes_accessed=2 * slots * side * side,
        transcendentals=0,
    )
    params = pltpu.CompilerParams(vmem_limit_bytes=VMEM_LIMIT)
    if activations is None:
        return pl.pallas_call(
            forward_kernel,
            out_shape=jax.ShapeDtypeStruct((n_targets, width, side), BF16),
            in_specs=[smem, smem, smem, vmem, vmem],
            out_specs=vmem,
            scratch_shapes=[pltpu.VMEM((n_targets + 1, width, side), F32)],
            compiler_params=params,
            cost_estimate=cost,
            name="tiles_forward",
        )(live, rows, cols, values, source)
    return pl.pallas_call(
        backward_kernel,
        out_shape=(
            jax.ShapeDtypeStruct((n_targets + 1, width, side), F32),
            jax.ShapeDtypeStruct(activations.shape, BF16),
        ),
        in_specs=[smem, smem, smem, vmem, vmem, vmem],
        out_specs=(vmem, pl.BlockSpec(memory_space=pl.ANY)),
        scratch_shapes=[pltpu.SemaphoreType.DMA],
        compiler_params=params,
        cost_estimate=cost,
        name="tiles_backward",
    )(live, rows, cols, values, source, activations)


def node_kernel(
    n_row, n_col,
    part_ref, weight_ref, cot_ref,
    act_ref, grads_ref, chunk_ref,
    came, wgrad, wcame,
    a_send, a_recv, g_send, g_recv, w_send, w_recv,
):
    row, col = lax.axis_index("row"), lax.axis_index("col")
    across = [{"col": lax.rem(col + d, n_col)} for d in range(1, n_col)]
    along = [lax.rem(row + d, n_row) for d in range(1, n_row)]
    ready = greet(across + [{"row": r} for r in along])
    ready()
    tiles = part_ref.shape[1]
    half = tiles // PIECES
    copies = []
    arrivals = []
    for q in range(PIECES):
        piece = pl.ds(q * half, half)
        for d in range(1, n_col):
            copy = remote(
                part_ref.at[lax.rem(col + d, n_col), piece], came.at[d - 1, piece],
                a_send.at[d - 1, q], a_recv.at[d - 1, q], across[d - 1],
            )
            copy.start()
            copies.append(copy)
            arrivals.append(copy)
    weight = weight_ref[...]
    total = None
    for q in range(PIECES):
        for copy in arrivals[q * (n_col - 1) : (q + 1) * (n_col - 1)]:
            copy.wait_recv()
        for t in range(q * half, (q + 1) * half):
            agg = part_ref[col, t].astype(F32)
            for d in range(1, n_col):
                agg += came[d - 1, t].astype(F32)
            low = agg.astype(BF16)
            nodes = slice(t * 128, (t + 1) * 128)
            pre = jnp.dot(agg.T.astype(BF16), weight, preferred_element_type=F32)
            sigma = 1.0 / (1.0 + jnp.exp(-pre))
            act_ref[nodes, :] = (pre * sigma).astype(BF16)
            cot = cot_ref[nodes, :].astype(F32)
            pre_grad = (cot * sigma * (1.0 + pre * (1.0 - sigma))).astype(BF16)
            grads_ref[col, t] = dot(weight, pre_grad, 1, 1).astype(BF16)
            term = jnp.dot(low, pre_grad, preferred_element_type=F32)
            total = term if total is None else total + term
        mine = grads_ref.at[col, pl.ds(q * half, half)]
        for d in range(1, n_col):
            copy = remote(mine, mine, g_send.at[d - 1, q], g_recv.at[d - 1, q], across[d - 1])
            copy.start()
            copies.append(copy)
    depth = wgrad.shape[1]
    for r in range(n_row):
        wgrad[r] = total[r * depth : (r + 1) * depth]
    w_copies = []
    for d in range(1, n_row):
        r = along[d - 1]
        copy = remote(wgrad.at[r], wcame.at[d - 1], w_send.at[d - 1], w_recv.at[d - 1], {"row": r})
        copy.start()
        w_copies.append(copy)
    for copy in w_copies:
        copy.wait_recv()
    chunk = wgrad[row]
    for d in range(1, n_row):
        chunk += wcame[d - 1]
    chunk_ref[...] = chunk
    for q in range(PIECES):
        for d in range(1, n_col):
            theirs = grads_ref.at[lax.rem(col + n_col - d, n_col), pl.ds(q * half, half)]
            remote(theirs, theirs, g_send.at[d - 1, q], g_recv.at[d - 1, q], across[d - 1]).wait_recv()
    for copy in copies + w_copies:
        copy.wait_send()


def node_step(part, weight, cotangent, n_row, n_col):
    _, tiles, width, side = part.shape
    hidden = weight.shape[1]
    depth = width // n_row
    vmem = pl.BlockSpec(memory_space=pltpu.VMEM)
    dma = pltpu.SemaphoreType.DMA
    return pl.pallas_call(
        functools.partial(node_kernel, n_row, n_col),
        out_shape=(
            jax.ShapeDtypeStruct(cotangent.shape, BF16),
            jax.ShapeDtypeStruct(part.shape, BF16),
            jax.ShapeDtypeStruct((depth, hidden), F32),
        ),
        in_specs=[vmem, vmem, vmem],
        out_specs=(vmem, vmem, vmem),
        scratch_shapes=[
            pltpu.VMEM((n_col - 1, tiles, width, side), BF16),
            pltpu.VMEM((n_row, depth, hidden), F32),
            pltpu.VMEM((n_row - 1, depth, hidden), F32),
            dma((n_col - 1, PIECES)),
            dma((n_col - 1, PIECES)),
            dma((n_col - 1, PIECES)),
            dma((n_col - 1, PIECES)),
            dma((n_row - 1,)),
            dma((n_row - 1,)),
        ],
        compiler_params=pltpu.CompilerParams(
            collective_id=1, has_side_effects=True, vmem_limit_bytes=VMEM_LIMIT
        ),
        name="node_step",
    )(part, weight, cotangent)


def scatter_kernel(
    n_row, n_col,
    part_ref, chunk_ref,
    out_ref, wgrad_ref,
    other, leaving, came, total_ref, wcols, wsum,
    p_send, p_recv, l_send, l_recv, c_send, c_recv, w_send, w_recv,
):
    chips = n_row // 2
    row, col = lax.axis_index("row"), lax.axis_index("col")
    chip, core = row // 2, row % 2
    partner = {"row": chip * 2 + 1 - core}
    along = [lax.rem(row + d, n_row) for d in range(1, n_row)]
    across = [{"col": lax.rem(col + d, n_col)} for d in range(1, n_col)]
    ready = greet([{"row": r} for r in along] + across)
    ready()
    tiles = came.shape[2]
    half = tiles // PIECES
    sides = ((0, 1), (1, -1))
    order = [(side, sign, hop) for hop in range(chips - 1, 0, -1) for side, sign in sides]

    def pair(side, hop, q, to_chip):
        piece = pl.ds(q * half, half)
        first = (to_chip * 2 + 1 - core) * tiles + q * half
        return remote(
            part_ref.at[pl.ds(first, half)], other.at[side, hop, piece],
            p_send.at[side, hop, q], p_recv.at[side, hop, q], partner,
        )

    def lane(side, hop, q, sign):
        piece = pl.ds(q * half, half)
        return remote(
            leaving.at[side, hop - 1, piece], came.at[side, hop - 1, piece],
            l_send.at[side, hop - 1, q], l_recv.at[side, hop - 1, q],
            {"row": row + 2 * sign},
        )

    for side, sign, hop in order:
        @pl.when(inside(chip + sign * hop, chips))
        def _():
            for q in range(PIECES):
                pair(side, hop, q, chip + sign * hop).start()
    for q in range(PIECES):
        pair(0, 0, q, chip).start()
    copies = []
    for d in range(1, n_col):
        copy = remote(chunk_ref, wcols.at[col], c_send.at[d - 1], c_recv.at[d - 1], across[d - 1])
        copy.start()
        copies.append(copy)
    wcols[col] = chunk_ref[...]

    def share_weight_grad():
        for d in range(1, n_col):
            source = lax.rem(col + n_col - d, n_col)
            remote(chunk_ref, wcols.at[source], c_send.at[d - 1], c_recv.at[d - 1], across[d - 1]).wait_recv()
        total = wcols[0]
        for c in range(1, n_col):
            total += wcols[c]
        wsum[...] = total
        wgrad_ref[row] = total
        for d in range(1, n_row):
            copy = remote(wsum, wgrad_ref.at[row], w_send.at[d - 1], w_recv.at[d - 1], {"row": along[d - 1]})
            copy.start()
            copies.append(copy)

    for hop in range(chips - 1, 0, -1):
        for q in range(PIECES):
            for side, sign in sides:
                to_chip = chip + sign * hop
                goes = inside(to_chip, chips)

                @pl.when(goes)
                def _():
                    pair(side, hop, q, to_chip).wait_recv()
                    for t in range(q * half, (q + 1) * half):
                        total_ref[t] = part_ref[(to_chip * 2 + core) * tiles + t] + other[side, hop, t]

                if hop + 1 < chips:
                    @pl.when(goes & inside(chip - sign, chips))
                    def _():
                        lane(side, hop + 1, q, sign).wait_recv()
                        for t in range(q * half, (q + 1) * half):
                            total_ref[t] = total_ref[t] + came[side, hop, t].astype(F32)

                @pl.when(goes)
                def _():
                    for t in range(q * half, (q + 1) * half):
                        leaving[side, hop - 1, t] = total_ref[t].astype(BF16)
                    lane(side, hop, q, sign).start()
        if hop == max(1, chips - 2):
            share_weight_grad()
    for q in range(PIECES):
        pair(0, 0, q, chip).wait_recv()
        for t in range(q * half, (q + 1) * half):
            total_ref[t] = part_ref[row * tiles + t] + other[0, 0, t]
        for side, sign in sides:
            @pl.when(inside(chip - sign, chips))
            def _():
                lane(side, 1, q, sign).wait_recv()
                for t in range(q * half, (q + 1) * half):
                    total_ref[t] = total_ref[t] + came[side, 0, t].astype(F32)
        for t in range(q * half, (q + 1) * half):
            out_ref[:, t * 128 : (t + 1) * 128] = total_ref[t].astype(BF16)
    for d in range(1, n_row):
        source = lax.rem(row + n_row - d, n_row)
        remote(wsum, wgrad_ref.at[source], w_send.at[d - 1], w_recv.at[d - 1], partner).wait_recv()
    for copy in copies:
        copy.wait_send()
    for q in range(PIECES):
        pair(0, 0, q, chip).wait_send()
        for side, sign, hop in order:
            @pl.when(inside(chip + sign * hop, chips))
            def _():
                pair(side, hop, q, chip + sign * hop).wait_send()
                lane(side, hop, q, sign).wait_send()


def scatter_step(part, chunk, tiles, n_row, n_col):
    _, width, side = part.shape
    depth, hidden = chunk.shape
    chips = n_row // 2
    vmem = pl.BlockSpec(memory_space=pltpu.VMEM)
    dma = pltpu.SemaphoreType.DMA
    return pl.pallas_call(
        functools.partial(scatter_kernel, n_row, n_col),
        out_shape=(
            jax.ShapeDtypeStruct((width, tiles * side), BF16),
            jax.ShapeDtypeStruct((n_row, depth, hidden), F32),
        ),
        in_specs=[vmem, vmem],
        out_specs=(vmem, vmem),
        scratch_shapes=[
            pltpu.VMEM((2, chips, tiles, width, side), F32),
            pltpu.VMEM((2, chips - 1, tiles, width, side), BF16),
            pltpu.VMEM((2, chips - 1, tiles, width, side), BF16),
            pltpu.VMEM((tiles, width, side), F32),
            pltpu.VMEM((n_col, depth, hidden), F32),
            pltpu.VMEM((depth, hidden), F32),
            dma((2, chips, PIECES)),
            dma((2, chips, PIECES)),
            dma((2, chips - 1, PIECES)),
            dma((2, chips - 1, PIECES)),
            dma((n_col - 1,)),
            dma((n_col - 1,)),
            dma((n_row - 1,)),
            dma((n_row - 1,)),
        ],
        compiler_params=pltpu.CompilerParams(
            collective_id=2, has_side_effects=True, vmem_limit_bytes=VMEM_LIMIT
        ),
        name="scatter_step",
    )(part, chunk)


def on_device(n_row, n_col, features, weight, cotangent, tile_values, tile_rows, tile_cols, tile_counts):
    own_rows, width = features.shape
    tiles = own_rows // 128
    sources, values = gather_features(features.T, tile_values[0, 0], n_row)
    sources = sources.reshape(n_row * tiles, width, 128)
    part = tile_pass(values, tile_rows, tile_cols, tile_counts, sources, n_col * tiles)
    activations, grads, chunk = node_step(
        part.reshape(n_col, tiles, width, 128), weight, cotangent, n_row, n_col
    )
    grads = grads.reshape(n_col * tiles, width, 128)
    grad_part, activations = tile_pass(
        values, tile_rows, tile_cols, tile_counts, grads, n_row * tiles, activations
    )
    out, weight_grad = scatter_step(grad_part, chunk, tiles, n_row, n_col)
    return activations, out.T, weight_grad.reshape(weight.shape)


def solution(mesh):
    in_specs = (
        P(("col", "row"), None),
        P(),
        P(("row", "col"), None),
        P("row", "col", None, None, None),
        P("row", "col", None),
        P("row", "col", None),
        P("row", "col"),
    )
    out_specs = (P(("row", "col"), None), P(("col", "row"), None), P())
    return jax.shard_map(
        functools.partial(on_device, mesh.shape["row"], mesh.shape["col"]),
        mesh=mesh,
        in_specs=in_specs,
        out_specs=out_specs,
        check_vma=False,
    )
```

```python
import functools

import jax
import jax.numpy as jnp
from jax import lax
from jax.experimental import pallas as pl
from jax.experimental.pallas import tpu as pltpu
from jax.sharding import PartitionSpec as P

MESH = pl.DeviceIdType.MESH
F32 = jnp.float32
BF16 = jnp.bfloat16
VMEM_LIMIT = 24 * 1024 * 1024
GATHER_VMEM_LIMIT = 39 * 1024 * 1024
PIECES = 4
GROUP = 32


def inside(chip, chips):
    return (chip >= 0) & (chip < chips)


def dot(a, b, contract_a, contract_b):
    return lax.dot_general(
        a, b, (((contract_a,), (contract_b,)), ((), ())), preferred_element_type=F32
    )


def greet(peers):
    barrier = pltpu.get_barrier_semaphore()
    for peer in peers:
        pl.semaphore_signal(barrier, inc=1, device_id=peer, device_id_type=MESH)
    return lambda: pl.semaphore_wait(barrier, len(peers))


def greet_line(chip, core, chips, peers):
    barrier = pltpu.get_barrier_semaphore()
    for peer in peers:
        pl.semaphore_signal(barrier, inc=1, device_id=peer, device_id_type=MESH)
    count = len(peers)
    for sign in (1, -1):
        there = inside(chip + sign, chips)
        count += there.astype(jnp.int32)

        @pl.when(there)
        def _():
            pl.semaphore_signal(
                barrier, inc=1, device_id={"row": (chip + sign) * 2 + core}, device_id_type=MESH
            )

    return lambda: pl.semaphore_wait(barrier, count)


def remote(src, dst, send_sem, recv_sem, peer):
    return pltpu.make_async_remote_copy(
        src_ref=src,
        dst_ref=dst,
        send_sem=send_sem,
        recv_sem=recv_sem,
        device_id=peer,
        device_id_type=MESH,
    )


def gather_kernel(n_row, f_ref, values_ref, out_ref, kept_ref, own_sem, load_sem, l_send, l_recv, p_send, p_recv):
    chips = n_row // 2
    me = lax.axis_index("row")
    chip, core = me // 2, me % 2
    partner = {"row": chip * 2 + 1 - core}
    tiles = out_ref.shape[1]
    half = tiles // PIECES
    load = pltpu.make_async_copy(values_ref, kept_ref, load_sem)
    ready = greet_line(chip, core, chips, [partner])
    fetches = []
    for t in range(tiles):
        fetch = pltpu.make_async_copy(
            f_ref.at[:, pl.ds(t * 128, 128)], out_ref.at[me, t], own_sem.at[t]
        )
        fetch.start()
        fetches.append(fetch)
    load.start()
    for fetch in fetches:
        fetch.wait()
    ready()

    def block(source, q):
        return out_ref.at[source, pl.ds(q * half, half)]

    def lane(side, hop, q, source, sign):
        piece = block(source, q)
        return remote(
            piece, piece, l_send.at[side, hop - 1, q], l_recv.at[side, hop - 1, q],
            {"row": me + 2 * sign},
        )

    def across(side, hop, q, source):
        piece = block(source, q)
        return remote(piece, piece, p_send.at[side, hop, q], p_recv.at[side, hop, q], partner)

    sides = ((0, 1), (1, -1))
    for q in range(PIECES):
        for side, sign in sides:
            @pl.when(inside(chip + sign, chips))
            def _():
                lane(side, 1, q, me, sign).start()
        across(0, 0, q, me).start()
    for hop in range(1, chips):
        for q in range(PIECES):
            for side, sign in sides:
                source = me - 2 * sign * hop
                came = inside(chip - sign * hop, chips)

                @pl.when(came)
                def _():
                    lane(side, hop, q, source, sign).wait_recv()

                if hop + 1 < chips:
                    @pl.when(came & inside(chip + sign, chips))
                    def _():
                        lane(side, hop + 1, q, source, sign).start()

                @pl.when(came)
                def _():
                    across(side, hop, q, source).start()
    for q in range(PIECES):
        across(0, 0, q, chip * 2 + 1 - core).wait_recv()
        across(0, 0, q, me).wait_send()
        for side, sign in sides:
            @pl.when(inside(chip + sign, chips))
            def _():
                lane(side, 1, q, me, sign).wait_send()
    for hop in range(1, chips):
        for q in range(PIECES):
            for side, sign in sides:
                source = me - 2 * sign * hop
                came = inside(chip - sign * hop, chips)

                @pl.when(came)
                def _():
                    across(side, hop, q, (chip - sign * hop) * 2 + 1 - core).wait_recv()
                    across(side, hop, q, source).wait_send()

                if hop + 1 < chips:
                    @pl.when(came & inside(chip + sign, chips))
                    def _():
                        lane(side, hop + 1, q, source, sign).wait_send()
    load.wait()


def gather_features(features, values, n_row):
    width, rows = features.shape
    tiles = rows // 128
    chips = n_row // 2
    vmem = pl.BlockSpec(memory_space=pltpu.VMEM)
    dma = pltpu.SemaphoreType.DMA
    return pl.pallas_call(
        functools.partial(gather_kernel, n_row),
        out_shape=(
            jax.ShapeDtypeStruct((n_row, tiles, width, 128), BF16),
            jax.ShapeDtypeStruct(values.shape, BF16),
        ),
        in_specs=[pl.BlockSpec(memory_space=pl.ANY)] * 2,
        out_specs=(vmem, vmem),
        scratch_shapes=[
            dma((tiles,)),
            dma,
            dma((2, chips - 1, PIECES)),
            dma((2, chips - 1, PIECES)),
            dma((2, chips, PIECES)),
            dma((2, chips, PIECES)),
        ],
        compiler_params=pltpu.CompilerParams(
            collective_id=0, has_side_effects=True, vmem_limit_bytes=GATHER_VMEM_LIMIT
        ),
        name="gather_features",
    )(features, values)


def add_tiles(transpose, live_ref, targets_ref, picks_ref, values_ref, source_ref, even, odd):
    group = GROUP
    live = live_ref[0, 0]
    spare = even.shape[0] - 1
    even[...] = jnp.zeros_like(even)
    odd[...] = jnp.zeros_like(odd)

    def body(g, carry):
        for u in range(group):
            slot = g * group + u
            pick = picks_ref[0, 0, slot]
            target = jnp.where(slot < live, targets_ref[0, 0, slot], spare)
            product = dot(source_ref[pick], values_ref[slot], 1, 0 if transpose else 1)
            acc = odd if u % 2 else even
            acc[target] += product
        return carry

    groups = (live + group - 1) // group
    lax.fori_loop(0, groups, body, 0)


def forward_kernel(live_ref, rows_ref, cols_ref, values_ref, source_ref, out_ref, even, odd):
    add_tiles(False, live_ref, rows_ref, cols_ref, values_ref, source_ref, even, odd)
    n = out_ref.shape[0]
    out_ref[...] = (even[0:n] + odd[0:n]).astype(BF16)


def backward_kernel(
    live_ref, rows_ref, cols_ref, values_ref, source_ref, act_ref, out_ref, act_out_ref, even, odd, sem
):
    write = pltpu.make_async_copy(act_ref, act_out_ref, sem)
    write.start()
    add_tiles(True, live_ref, cols_ref, rows_ref, values_ref, source_ref, even, odd)
    n = out_ref.shape[0]
    out_ref[...] = even[0:n] + odd[0:n]
    write.wait()


def tile_pass(values, rows, cols, live, source, n_targets, activations=None):
    slots, side, _ = values.shape
    width = source.shape[1]
    smem = pl.BlockSpec(memory_space=pltpu.SMEM)
    vmem = pl.BlockSpec(memory_space=pltpu.VMEM)
    cost = pl.CostEstimate(
        flops=2 * slots * side * side * width,
        bytes_accessed=2 * slots * side * side,
        transcendentals=0,
    )
    params = pltpu.CompilerParams(vmem_limit_bytes=VMEM_LIMIT)
    totals = [pltpu.VMEM((n_targets + 1, width, side), F32)] * 2
    if activations is None:
        return pl.pallas_call(
            forward_kernel,
            out_shape=jax.ShapeDtypeStruct((n_targets, width, side), BF16),
            in_specs=[smem, smem, smem, vmem, vmem],
            out_specs=vmem,
            scratch_shapes=totals,
            compiler_params=params,
            cost_estimate=cost,
            name="tiles_forward",
        )(live, rows, cols, values, source)
    return pl.pallas_call(
        backward_kernel,
        out_shape=(
            jax.ShapeDtypeStruct((n_targets, width, side), F32),
            jax.ShapeDtypeStruct(activations.shape, BF16),
        ),
        in_specs=[smem, smem, smem, vmem, vmem, vmem],
        out_specs=(vmem, pl.BlockSpec(memory_space=pl.ANY)),
        scratch_shapes=totals + [pltpu.SemaphoreType.DMA],
        compiler_params=params,
        cost_estimate=cost,
        name="tiles_backward",
    )(live, rows, cols, values, source, activations)


def node_kernel(
    n_row, n_col,
    part_ref, weight_ref, cot_ref,
    act_ref, grads_ref, chunk_ref,
    came, wgrad, wcame,
    a_send, a_recv, g_send, g_recv, w_send, w_recv,
):
    row, col = lax.axis_index("row"), lax.axis_index("col")
    across = [{"col": lax.rem(col + d, n_col)} for d in range(1, n_col)]
    along = [lax.rem(row + d, n_row) for d in range(1, n_row)]
    ready = greet(across + [{"row": r} for r in along])
    ready()
    tiles = part_ref.shape[1]
    half = tiles // PIECES
    copies = []
    arrivals = []
    for q in range(PIECES):
        piece = pl.ds(q * half, half)
        for d in range(1, n_col):
            copy = remote(
                part_ref.at[lax.rem(col + d, n_col), piece], came.at[d - 1, piece],
                a_send.at[d - 1, q], a_recv.at[d - 1, q], across[d - 1],
            )
            copy.start()
            copies.append(copy)
            arrivals.append(copy)
    weight = weight_ref[...]
    total = None
    for q in range(PIECES):
        for copy in arrivals[q * (n_col - 1) : (q + 1) * (n_col - 1)]:
            copy.wait_recv()
        for t in range(q * half, (q + 1) * half):
            agg = part_ref[col, t].astype(F32)
            for d in range(1, n_col):
                agg += came[d - 1, t].astype(F32)
            low = agg.astype(BF16)
            nodes = slice(t * 128, (t + 1) * 128)
            pre = jnp.dot(agg.T.astype(BF16), weight, preferred_element_type=F32)
            sigma = 1.0 / (1.0 + jnp.exp(-pre))
            act_ref[nodes, :] = (pre * sigma).astype(BF16)
            cot = cot_ref[nodes, :].astype(F32)
            pre_grad = (cot * sigma * (1.0 + pre * (1.0 - sigma))).astype(BF16)
            grads_ref[col, t] = dot(weight, pre_grad, 1, 1).astype(BF16)
            term = jnp.dot(low, pre_grad, preferred_element_type=F32)
            total = term if total is None else total + term
        mine = grads_ref.at[col, pl.ds(q * half, half)]
        for d in range(1, n_col):
            copy = remote(mine, mine, g_send.at[d - 1, q], g_recv.at[d - 1, q], across[d - 1])
            copy.start()
            copies.append(copy)
    depth = wgrad.shape[1]
    for r in range(n_row):
        wgrad[r] = total[r * depth : (r + 1) * depth]
    w_copies = []
    for d in range(1, n_row):
        r = along[d - 1]
        copy = remote(wgrad.at[r], wcame.at[d - 1], w_send.at[d - 1], w_recv.at[d - 1], {"row": r})
        copy.start()
        w_copies.append(copy)
    for copy in w_copies:
        copy.wait_recv()
    chunk = wgrad[row]
    for d in range(1, n_row):
        chunk += wcame[d - 1]
    chunk_ref[...] = chunk
    for q in range(PIECES):
        for d in range(1, n_col):
            theirs = grads_ref.at[lax.rem(col + n_col - d, n_col), pl.ds(q * half, half)]
            remote(theirs, theirs, g_send.at[d - 1, q], g_recv.at[d - 1, q], across[d - 1]).wait_recv()
    for copy in copies + w_copies:
        copy.wait_send()


def node_step(part, weight, cotangent, n_row, n_col):
    _, tiles, width, side = part.shape
    hidden = weight.shape[1]
    depth = width // n_row
    vmem = pl.BlockSpec(memory_space=pltpu.VMEM)
    dma = pltpu.SemaphoreType.DMA
    return pl.pallas_call(
        functools.partial(node_kernel, n_row, n_col),
        out_shape=(
            jax.ShapeDtypeStruct(cotangent.shape, BF16),
            jax.ShapeDtypeStruct(part.shape, BF16),
            jax.ShapeDtypeStruct((depth, hidden), F32),
        ),
        in_specs=[vmem, vmem, vmem],
        out_specs=(vmem, vmem, vmem),
        scratch_shapes=[
            pltpu.VMEM((n_col - 1, tiles, width, side), BF16),
            pltpu.VMEM((n_row, depth, hidden), F32),
            pltpu.VMEM((n_row - 1, depth, hidden), F32),
            dma((n_col - 1, PIECES)),
            dma((n_col - 1, PIECES)),
            dma((n_col - 1, PIECES)),
            dma((n_col - 1, PIECES)),
            dma((n_row - 1,)),
            dma((n_row - 1,)),
        ],
        compiler_params=pltpu.CompilerParams(
            collective_id=1, has_side_effects=True, vmem_limit_bytes=VMEM_LIMIT
        ),
        name="node_step",
    )(part, weight, cotangent)


def scatter_kernel(
    n_row, n_col,
    part_ref, chunk_ref,
    out_ref, wgrad_ref,
    other, leaving, came, total_ref, wcols, wsum,
    p_send, p_recv, l_send, l_recv, c_send, c_recv, w_send, w_recv,
):
    chips = n_row // 2
    row, col = lax.axis_index("row"), lax.axis_index("col")
    chip, core = row // 2, row % 2
    partner = {"row": chip * 2 + 1 - core}
    along = [lax.rem(row + d, n_row) for d in range(1, n_row)]
    across = [{"col": lax.rem(col + d, n_col)} for d in range(1, n_col)]
    ready = greet([{"row": r} for r in along] + across)
    ready()
    tiles = came.shape[2]
    half = tiles // PIECES
    sides = ((0, 1), (1, -1))
    order = [(side, sign, hop) for hop in range(chips - 1, 0, -1) for side, sign in sides]

    def pair(side, hop, q, to_chip):
        piece = pl.ds(q * half, half)
        first = (to_chip * 2 + 1 - core) * tiles + q * half
        return remote(
            part_ref.at[pl.ds(first, half)], other.at[side, hop, piece],
            p_send.at[side, hop, q], p_recv.at[side, hop, q], partner,
        )

    def lane(side, hop, q, sign):
        piece = pl.ds(q * half, half)
        return remote(
            leaving.at[side, hop - 1, piece], came.at[side, hop - 1, piece],
            l_send.at[side, hop - 1, q], l_recv.at[side, hop - 1, q],
            {"row": row + 2 * sign},
        )

    for side, sign, hop in order:
        @pl.when(inside(chip + sign * hop, chips))
        def _():
            for q in range(PIECES):
                pair(side, hop, q, chip + sign * hop).start()
    for q in range(PIECES):
        pair(0, 0, q, chip).start()
    copies = []
    for d in range(1, n_col):
        copy = remote(chunk_ref, wcols.at[col], c_send.at[d - 1], c_recv.at[d - 1], across[d - 1])
        copy.start()
        copies.append(copy)
    wcols[col] = chunk_ref[...]

    def share_weight_grad():
        for d in range(1, n_col):
            source = lax.rem(col + n_col - d, n_col)
            remote(chunk_ref, wcols.at[source], c_send.at[d - 1], c_recv.at[d - 1], across[d - 1]).wait_recv()
        total = wcols[0]
        for c in range(1, n_col):
            total += wcols[c]
        wsum[...] = total
        wgrad_ref[row] = total
        for d in range(1, n_row):
            copy = remote(wsum, wgrad_ref.at[row], w_send.at[d - 1], w_recv.at[d - 1], {"row": along[d - 1]})
            copy.start()
            copies.append(copy)

    for hop in range(chips - 1, 0, -1):
        for q in range(PIECES):
            for side, sign in sides:
                to_chip = chip + sign * hop
                goes = inside(to_chip, chips)

                @pl.when(goes)
                def _():
                    pair(side, hop, q, to_chip).wait_recv()
                    for t in range(q * half, (q + 1) * half):
                        total_ref[t] = part_ref[(to_chip * 2 + core) * tiles + t] + other[side, hop, t]

                if hop + 1 < chips:
                    @pl.when(goes & inside(chip - sign, chips))
                    def _():
                        lane(side, hop + 1, q, sign).wait_recv()
                        for t in range(q * half, (q + 1) * half):
                            total_ref[t] = total_ref[t] + came[side, hop, t].astype(F32)

                @pl.when(goes)
                def _():
                    for t in range(q * half, (q + 1) * half):
                        leaving[side, hop - 1, t] = total_ref[t].astype(BF16)
                    lane(side, hop, q, sign).start()
        if hop == max(1, chips - 2):
            share_weight_grad()
    for q in range(PIECES):
        pair(0, 0, q, chip).wait_recv()
        for t in range(q * half, (q + 1) * half):
            total_ref[t] = part_ref[row * tiles + t] + other[0, 0, t]
        for side, sign in sides:
            @pl.when(inside(chip - sign, chips))
            def _():
                lane(side, 1, q, sign).wait_recv()
                for t in range(q * half, (q + 1) * half):
                    total_ref[t] = total_ref[t] + came[side, 0, t].astype(F32)
        for t in range(q * half, (q + 1) * half):
            out_ref[:, t * 128 : (t + 1) * 128] = total_ref[t].astype(BF16)
    for d in range(1, n_row):
        source = lax.rem(row + n_row - d, n_row)
        remote(wsum, wgrad_ref.at[source], w_send.at[d - 1], w_recv.at[d - 1], partner).wait_recv()
    for copy in copies:
        copy.wait_send()
    for q in range(PIECES):
        pair(0, 0, q, chip).wait_send()
        for side, sign, hop in order:
            @pl.when(inside(chip + sign * hop, chips))
            def _():
                pair(side, hop, q, chip + sign * hop).wait_send()
                lane(side, hop, q, sign).wait_send()


def scatter_step(part, chunk, tiles, n_row, n_col):
    _, width, side = part.shape
    depth, hidden = chunk.shape
    chips = n_row // 2
    vmem = pl.BlockSpec(memory_space=pltpu.VMEM)
    dma = pltpu.SemaphoreType.DMA
    return pl.pallas_call(
        functools.partial(scatter_kernel, n_row, n_col),
        out_shape=(
            jax.ShapeDtypeStruct((width, tiles * side), BF16),
            jax.ShapeDtypeStruct((n_row, depth, hidden), F32),
        ),
        in_specs=[vmem, vmem],
        out_specs=(vmem, vmem),
        scratch_shapes=[
            pltpu.VMEM((2, chips, tiles, width, side), F32),
            pltpu.VMEM((2, chips - 1, tiles, width, side), BF16),
            pltpu.VMEM((2, chips - 1, tiles, width, side), BF16),
            pltpu.VMEM((tiles, width, side), F32),
            pltpu.VMEM((n_col, depth, hidden), F32),
            pltpu.VMEM((depth, hidden), F32),
            dma((2, chips, PIECES)),
            dma((2, chips, PIECES)),
            dma((2, chips - 1, PIECES)),
            dma((2, chips - 1, PIECES)),
            dma((n_col - 1,)),
            dma((n_col - 1,)),
            dma((n_row - 1,)),
            dma((n_row - 1,)),
        ],
        compiler_params=pltpu.CompilerParams(
            collective_id=2, has_side_effects=True, vmem_limit_bytes=VMEM_LIMIT
        ),
        name="scatter_step",
    )(part, chunk)


def on_device(n_row, n_col, features, weight, cotangent, tile_values, tile_rows, tile_cols, tile_counts):
    own_rows, width = features.shape
    tiles = own_rows // 128
    sources, values = gather_features(features.T, tile_values[0, 0], n_row)
    sources = sources.reshape(n_row * tiles, width, 128)
    part = tile_pass(values, tile_rows, tile_cols, tile_counts, sources, n_col * tiles)
    activations, grads, chunk = node_step(
        part.reshape(n_col, tiles, width, 128), weight, cotangent, n_row, n_col
    )
    grads = grads.reshape(n_col * tiles, width, 128)
    grad_part, activations = tile_pass(
        values, tile_rows, tile_cols, tile_counts, grads, n_row * tiles, activations
    )
    out, weight_grad = scatter_step(grad_part, chunk, tiles, n_row, n_col)
    return activations, out.T, weight_grad.reshape(weight.shape)


def solution(mesh):
    in_specs = (
        P(("col", "row"), None),
        P(),
        P(("row", "col"), None),
        P("row", "col", None, None, None),
        P("row", "col", None),
        P("row", "col", None),
        P("row", "col"),
    )
    out_specs = (P(("row", "col"), None), P(("col", "row"), None), P())
    return jax.shard_map(
        functools.partial(on_device, mesh.shape["row"], mesh.shape["col"]),
        mesh=mesh,
        in_specs=in_specs,
        out_specs=out_specs,
        check_vma=False,
    )
```

```python
import functools

import jax
import jax.numpy as jnp
from jax import lax
from jax.experimental import pallas as pl
from jax.experimental.pallas import tpu as pltpu
from jax.sharding import PartitionSpec as P

MESH = pl.DeviceIdType.MESH
F32 = jnp.float32
BF16 = jnp.bfloat16
VMEM_LIMIT = 14 * 1024 * 1024
GATHER_VMEM_LIMIT = 20 * 1024 * 1024
PIECES = 4
GROUP = 32
LOADS = 4
TURNS = 8


def inside(chip, chips):
    return (chip >= 0) & (chip < chips)


def dot(a, b, contract_a, contract_b):
    return lax.dot_general(
        a, b, (((contract_a,), (contract_b,)), ((), ())), preferred_element_type=F32
    )


def greet(peers):
    barrier = pltpu.get_barrier_semaphore()
    for peer in peers:
        pl.semaphore_signal(barrier, inc=1, device_id=peer, device_id_type=MESH)
    return lambda: pl.semaphore_wait(barrier, len(peers))


def greet_line(chip, core, chips, peers):
    barrier = pltpu.get_barrier_semaphore()
    for peer in peers:
        pl.semaphore_signal(barrier, inc=1, device_id=peer, device_id_type=MESH)
    count = len(peers)
    for sign in (1, -1):
        there = inside(chip + sign, chips)
        count += there.astype(jnp.int32)

        @pl.when(there)
        def _():
            pl.semaphore_signal(
                barrier, inc=1, device_id={"row": (chip + sign) * 2 + core}, device_id_type=MESH
            )

    return lambda: pl.semaphore_wait(barrier, count)


def remote(src, dst, send_sem, recv_sem, peer):
    return pltpu.make_async_remote_copy(
        src_ref=src,
        dst_ref=dst,
        send_sem=send_sem,
        recv_sem=recv_sem,
        device_id=peer,
        device_id_type=MESH,
    )


def gather_kernel(n_row, f_ref, values_ref, out_ref, kept_ref, turned_ref, own_sem, load_sem, l_send, l_recv, p_send, p_recv):
    chips = n_row // 2
    me = lax.axis_index("row")
    chip, core = me // 2, me % 2
    partner = {"row": chip * 2 + 1 - core}
    tiles = out_ref.shape[1]
    half = tiles // PIECES
    slots = kept_ref.shape[0]
    loads = []
    for i in range(LOADS):
        part = pl.ds(i * (slots // LOADS), slots // LOADS)
        loads.append(pltpu.make_async_copy(values_ref.at[part], kept_ref.at[part], load_sem.at[i]))
    ready = greet_line(chip, core, chips, [partner])
    fetches = []
    for t in range(tiles):
        fetch = pltpu.make_async_copy(
            f_ref.at[:, pl.ds(t * 128, 128)], out_ref.at[me, t], own_sem.at[t]
        )
        fetch.start()
        fetches.append(fetch)
    for load in loads:
        load.start()
    for fetch in fetches:
        fetch.wait()
    ready()

    def block(source, q):
        return out_ref.at[source, pl.ds(q * half, half)]

    def lane(side, hop, q, source, sign):
        piece = block(source, q)
        return remote(
            piece, piece, l_send.at[side, hop - 1, q], l_recv.at[side, hop - 1, q],
            {"row": me + 2 * sign},
        )

    def across(side, hop, q, source):
        piece = block(source, q)
        return remote(piece, piece, p_send.at[side, hop, q], p_recv.at[side, hop, q], partner)

    sides = ((0, 1), (1, -1))
    for q in range(PIECES):
        for side, sign in sides:
            @pl.when(inside(chip + sign, chips))
            def _():
                lane(side, 1, q, me, sign).start()
        across(0, 0, q, me).start()
    def turn(i, carry):
        for u in range(TURNS):
            turned_ref[i * TURNS + u] = kept_ref[i * TURNS + u].T
        return carry

    waited = 0
    rounds = (chips - 1) * PIECES
    for hop in range(1, chips):
        for q in range(PIECES):
            now = (hop - 1) * PIECES + q
            first, last = (slots // TURNS * n // rounds for n in (now, now + 1))
            while waited < LOADS and waited * (slots // LOADS) < last * TURNS:
                loads[waited].wait()
                waited += 1
            lax.fori_loop(first, last, turn, 0)
            for side, sign in sides:
                source = me - 2 * sign * hop
                came = inside(chip - sign * hop, chips)

                @pl.when(came)
                def _():
                    lane(side, hop, q, source, sign).wait_recv()

                if hop + 1 < chips:
                    @pl.when(came & inside(chip + sign, chips))
                    def _():
                        lane(side, hop + 1, q, source, sign).start()

                @pl.when(came)
                def _():
                    across(side, hop, q, source).start()
    for q in range(PIECES):
        across(0, 0, q, chip * 2 + 1 - core).wait_recv()
        across(0, 0, q, me).wait_send()
        for side, sign in sides:
            @pl.when(inside(chip + sign, chips))
            def _():
                lane(side, 1, q, me, sign).wait_send()
    for hop in range(1, chips):
        for q in range(PIECES):
            for side, sign in sides:
                source = me - 2 * sign * hop
                came = inside(chip - sign * hop, chips)

                @pl.when(came)
                def _():
                    across(side, hop, q, (chip - sign * hop) * 2 + 1 - core).wait_recv()
                    across(side, hop, q, source).wait_send()

                if hop + 1 < chips:
                    @pl.when(came & inside(chip + sign, chips))
                    def _():
                        lane(side, hop + 1, q, source, sign).wait_send()


def gather_features(features, values, n_row):
    width, rows = features.shape
    tiles = rows // 128
    chips = n_row // 2
    vmem = pl.BlockSpec(memory_space=pltpu.VMEM)
    dma = pltpu.SemaphoreType.DMA
    return pl.pallas_call(
        functools.partial(gather_kernel, n_row),
        out_shape=(
            jax.ShapeDtypeStruct((n_row, tiles, width, 128), BF16),
            jax.ShapeDtypeStruct(values.shape, BF16),
            jax.ShapeDtypeStruct(values.shape, BF16),
        ),
        in_specs=[pl.BlockSpec(memory_space=pl.ANY)] * 2,
        out_specs=(vmem, vmem, vmem),
        scratch_shapes=[
            dma((tiles,)),
            dma((LOADS,)),
            dma((2, chips - 1, PIECES)),
            dma((2, chips - 1, PIECES)),
            dma((2, chips, PIECES)),
            dma((2, chips, PIECES)),
        ],
        compiler_params=pltpu.CompilerParams(
            collective_id=0, has_side_effects=True, vmem_limit_bytes=GATHER_VMEM_LIMIT
        ),
        name="gather_features",
    )(features, values)


def add_tiles(live_ref, targets_ref, picks_ref, values_ref, source_ref, even, odd):
    group = GROUP
    live = live_ref[0, 0]
    spare = even.shape[0] - 1
    even[...] = jnp.zeros_like(even)
    odd[...] = jnp.zeros_like(odd)

    def body(g, carry):
        for u in range(group):
            slot = g * group + u
            pick = picks_ref[0, 0, slot]
            target = jnp.where(slot < live, targets_ref[0, 0, slot], spare)
            product = dot(source_ref[pick], values_ref[slot], 1, 0)
            acc = odd if u % 2 else even
            acc[target] += product
        return carry

    groups = (live + group - 1) // group
    lax.fori_loop(0, groups, body, 0)


def forward_kernel(live_ref, rows_ref, cols_ref, values_ref, source_ref, out_ref, even, odd):
    add_tiles(live_ref, rows_ref, cols_ref, values_ref, source_ref, even, odd)
    n = out_ref.shape[0]
    out_ref[...] = (even[0:n] + odd[0:n]).astype(BF16)


def backward_kernel(
    live_ref, rows_ref, cols_ref, values_ref, source_ref, act_ref, out_ref, act_out_ref, even, odd, sem
):
    write = pltpu.make_async_copy(act_ref, act_out_ref, sem)
    write.start()
    add_tiles(live_ref, cols_ref, rows_ref, values_ref, source_ref, even, odd)
    n = out_ref.shape[0]
    out_ref[...] = even[0:n] + odd[0:n]
    write.wait()


def tile_pass(values, rows, cols, live, source, n_targets, activations=None):
    slots, side, _ = values.shape
    width = source.shape[1]
    smem = pl.BlockSpec(memory_space=pltpu.SMEM)
    vmem = pl.BlockSpec(memory_space=pltpu.VMEM)
    cost = pl.CostEstimate(
        flops=2 * slots * side * side * width,
        bytes_accessed=2 * slots * side * side,
        transcendentals=0,
    )
    params = pltpu.CompilerParams(vmem_limit_bytes=VMEM_LIMIT)
    totals = [pltpu.VMEM((n_targets + 1, width, side), F32)] * 2
    if activations is None:
        return pl.pallas_call(
            forward_kernel,
            out_shape=jax.ShapeDtypeStruct((n_targets, width, side), BF16),
            in_specs=[smem, smem, smem, vmem, vmem],
            out_specs=vmem,
            scratch_shapes=totals,
            compiler_params=params,
            cost_estimate=cost,
            name="tiles_forward",
        )(live, rows, cols, values, source)
    return pl.pallas_call(
        backward_kernel,
        out_shape=(
            jax.ShapeDtypeStruct((n_targets, width, side), F32),
            jax.ShapeDtypeStruct(activations.shape, BF16),
        ),
        in_specs=[smem, smem, smem, vmem, vmem, vmem],
        out_specs=(vmem, pl.BlockSpec(memory_space=pl.ANY)),
        scratch_shapes=totals + [pltpu.SemaphoreType.DMA],
        compiler_params=params,
        cost_estimate=cost,
        name="tiles_backward",
    )(live, rows, cols, values, source, activations)


def node_kernel(
    n_row, n_col,
    part_ref, weight_ref, cot_ref,
    act_ref, grads_ref, wgrad_ref,
    came, a_send, a_recv, g_send, g_recv,
):
    col = lax.axis_index("col")
    across = [{"col": lax.rem(col + d, n_col)} for d in range(1, n_col)]
    ready = greet(across)
    ready()
    tiles = part_ref.shape[1]
    half = tiles // PIECES
    copies = []
    arrivals = []
    for q in range(PIECES):
        piece = pl.ds(q * half, half)
        for d in range(1, n_col):
            copy = remote(
                part_ref.at[lax.rem(col + d, n_col), piece], came.at[d - 1, piece],
                a_send.at[d - 1, q], a_recv.at[d - 1, q], across[d - 1],
            )
            copy.start()
            copies.append(copy)
            arrivals.append(copy)
    weight = weight_ref[...]
    total = None
    for q in range(PIECES):
        for copy in arrivals[q * (n_col - 1) : (q + 1) * (n_col - 1)]:
            copy.wait_recv()
        for t in range(q * half, (q + 1) * half):
            agg = part_ref[col, t].astype(F32)
            for d in range(1, n_col):
                agg += came[d - 1, t].astype(F32)
            low = agg.astype(BF16)
            nodes = slice(t * 128, (t + 1) * 128)
            pre = jnp.dot(agg.T.astype(BF16), weight, preferred_element_type=F32)
            sigma = 1.0 / (1.0 + jnp.exp(-pre))
            act_ref[nodes, :] = (pre * sigma).astype(BF16)
            cot = cot_ref[nodes, :].astype(F32)
            pre_grad = (cot * sigma * (1.0 + pre * (1.0 - sigma))).astype(BF16)
            grads_ref[col, t] = dot(weight, pre_grad, 1, 1).astype(BF16)
            term = jnp.dot(low, pre_grad, preferred_element_type=F32)
            total = term if total is None else total + term
        mine = grads_ref.at[col, pl.ds(q * half, half)]
        for d in range(1, n_col):
            copy = remote(mine, mine, g_send.at[d - 1, q], g_recv.at[d - 1, q], across[d - 1])
            copy.start()
            copies.append(copy)
    depth = wgrad_ref.shape[1]
    for r in range(n_row):
        wgrad_ref[r] = total[r * depth : (r + 1) * depth]
    for q in range(PIECES):
        for d in range(1, n_col):
            theirs = grads_ref.at[lax.rem(col + n_col - d, n_col), pl.ds(q * half, half)]
            remote(theirs, theirs, g_send.at[d - 1, q], g_recv.at[d - 1, q], across[d - 1]).wait_recv()
    for copy in copies:
        copy.wait_send()


def node_step(part, weight, cotangent, n_row, n_col):
    _, tiles, width, side = part.shape
    hidden = weight.shape[1]
    depth = width // n_row
    vmem = pl.BlockSpec(memory_space=pltpu.VMEM)
    dma = pltpu.SemaphoreType.DMA
    return pl.pallas_call(
        functools.partial(node_kernel, n_row, n_col),
        out_shape=(
            jax.ShapeDtypeStruct(cotangent.shape, BF16),
            jax.ShapeDtypeStruct(part.shape, BF16),
            jax.ShapeDtypeStruct((n_row, depth, hidden), F32),
        ),
        in_specs=[vmem, vmem, vmem],
        out_specs=(vmem, vmem, vmem),
        scratch_shapes=[
            pltpu.VMEM((n_col - 1, tiles, width, side), BF16),
            dma((n_col - 1, PIECES)),
            dma((n_col - 1, PIECES)),
            dma((n_col - 1, PIECES)),
            dma((n_col - 1, PIECES)),
        ],
        compiler_params=pltpu.CompilerParams(
            collective_id=1, has_side_effects=True, vmem_limit_bytes=VMEM_LIMIT
        ),
        name="node_step",
    )(part, weight, cotangent)


def scatter_kernel(
    n_row, n_col,
    part_ref, term_ref,
    out_ref, wgrad_ref,
    other, leaving, came, total_ref, wrows, wcols, wsum,
    p_send, p_recv, l_send, l_recv, r_send, r_recv, c_send, c_recv, w_send, w_recv,
):
    chips = n_row // 2
    row, col = lax.axis_index("row"), lax.axis_index("col")
    chip, core = row // 2, row % 2
    partner = {"row": chip * 2 + 1 - core}
    along = [lax.rem(row + d, n_row) for d in range(1, n_row)]
    across = [{"col": lax.rem(col + d, n_col)} for d in range(1, n_col)]
    ready = greet([{"row": r} for r in along] + across)
    ready()
    tiles = came.shape[2]
    half = tiles // PIECES
    sides = ((0, 1), (1, -1))
    order = [(side, sign, hop) for hop in range(chips - 1, 0, -1) for side, sign in sides]

    def pair(side, hop, q, to_chip):
        piece = pl.ds(q * half, half)
        first = (to_chip * 2 + 1 - core) * tiles + q * half
        return remote(
            part_ref.at[pl.ds(first, half)], other.at[side, hop, piece],
            p_send.at[side, hop, q], p_recv.at[side, hop, q], partner,
        )

    def lane(side, hop, q, sign):
        piece = pl.ds(q * half, half)
        return remote(
            leaving.at[side, hop - 1, piece], came.at[side, hop - 1, piece],
            l_send.at[side, hop - 1, q], l_recv.at[side, hop - 1, q],
            {"row": row + 2 * sign},
        )

    for side, sign, hop in order:
        @pl.when(inside(chip + sign * hop, chips))
        def _():
            for q in range(PIECES):
                pair(side, hop, q, chip + sign * hop).start()
    for q in range(PIECES):
        pair(0, 0, q, chip).start()
    copies = []
    arrivals = []
    for d in range(1, n_row):
        copy = remote(
            term_ref.at[along[d - 1]], wrows.at[d - 1], r_send.at[d - 1], r_recv.at[d - 1],
            {"row": along[d - 1]},
        )
        copy.start()
        copies.append(copy)
        arrivals.append(copy)

    def sum_rows():
        for copy in arrivals:
            copy.wait_recv()
        total = term_ref[row]
        for d in range(1, n_row):
            total += wrows[d - 1]
        wcols[col] = total
        for d in range(1, n_col):
            mine = wcols.at[col]
            copy = remote(mine, mine, c_send.at[d - 1], c_recv.at[d - 1], across[d - 1])
            copy.start()
            copies.append(copy)

    def sum_cols():
        for d in range(1, n_col):
            theirs = wcols.at[lax.rem(col + n_col - d, n_col)]
            remote(theirs, theirs, c_send.at[d - 1], c_recv.at[d - 1], across[d - 1]).wait_recv()
        total = wcols[0]
        for c in range(1, n_col):
            total += wcols[c]
        wsum[...] = total
        wgrad_ref[row] = total
        for d in range(1, n_row):
            copy = remote(wsum, wgrad_ref.at[row], w_send.at[d - 1], w_recv.at[d - 1], {"row": along[d - 1]})
            copy.start()
            copies.append(copy)

    for hop in range(chips - 1, 0, -1):
        for q in range(PIECES):
            for side, sign in sides:
                to_chip = chip + sign * hop
                goes = inside(to_chip, chips)

                @pl.when(goes)
                def _():
                    pair(side, hop, q, to_chip).wait_recv()
                    for t in range(q * half, (q + 1) * half):
                        total_ref[t] = part_ref[(to_chip * 2 + core) * tiles + t] + other[side, hop, t]

                if hop + 1 < chips:
                    @pl.when(goes & inside(chip - sign, chips))
                    def _():
                        lane(side, hop + 1, q, sign).wait_recv()
                        for t in range(q * half, (q + 1) * half):
                            total_ref[t] = total_ref[t] + came[side, hop, t].astype(F32)

                @pl.when(goes)
                def _():
                    for t in range(q * half, (q + 1) * half):
                        leaving[side, hop - 1, t] = total_ref[t].astype(BF16)
                    lane(side, hop, q, sign).start()
        if hop == chips - 1:
            sum_rows()
        if hop == max(1, chips - 2):
            sum_cols()
    for q in range(PIECES):
        pair(0, 0, q, chip).wait_recv()
        for t in range(q * half, (q + 1) * half):
            total_ref[t] = part_ref[row * tiles + t] + other[0, 0, t]
        for side, sign in sides:
            @pl.when(inside(chip - sign, chips))
            def _():
                lane(side, 1, q, sign).wait_recv()
                for t in range(q * half, (q + 1) * half):
                    total_ref[t] = total_ref[t] + came[side, 0, t].astype(F32)
        for t in range(q * half, (q + 1) * half):
            out_ref[:, t * 128 : (t + 1) * 128] = total_ref[t].astype(BF16)
    for d in range(1, n_row):
        source = lax.rem(row + n_row - d, n_row)
        remote(wsum, wgrad_ref.at[source], w_send.at[d - 1], w_recv.at[d - 1], partner).wait_recv()
    for copy in copies:
        copy.wait_send()
    for q in range(PIECES):
        pair(0, 0, q, chip).wait_send()
        for side, sign, hop in order:
            @pl.when(inside(chip + sign * hop, chips))
            def _():
                pair(side, hop, q, chip + sign * hop).wait_send()
                lane(side, hop, q, sign).wait_send()


def scatter_step(part, term, tiles, n_row, n_col):
    _, width, side = part.shape
    _, depth, hidden = term.shape
    chips = n_row // 2
    vmem = pl.BlockSpec(memory_space=pltpu.VMEM)
    dma = pltpu.SemaphoreType.DMA
    return pl.pallas_call(
        functools.partial(scatter_kernel, n_row, n_col),
        out_shape=(
            jax.ShapeDtypeStruct((width, tiles * side), BF16),
            jax.ShapeDtypeStruct((n_row, depth, hidden), F32),
        ),
        in_specs=[vmem, vmem],
        out_specs=(vmem, vmem),
        scratch_shapes=[
            pltpu.VMEM((2, chips, tiles, width, side), F32),
            pltpu.VMEM((2, chips - 1, tiles, width, side), BF16),
            pltpu.VMEM((2, chips - 1, tiles, width, side), BF16),
            pltpu.VMEM((tiles, width, side), F32),
            pltpu.VMEM((n_row - 1, depth, hidden), F32),
            pltpu.VMEM((n_col, depth, hidden), F32),
            pltpu.VMEM((depth, hidden), F32),
            dma((2, chips, PIECES)),
            dma((2, chips, PIECES)),
            dma((2, chips - 1, PIECES)),
            dma((2, chips - 1, PIECES)),
            dma((n_row - 1,)),
            dma((n_row - 1,)),
            dma((n_col - 1,)),
            dma((n_col - 1,)),
            dma((n_row - 1,)),
            dma((n_row - 1,)),
        ],
        compiler_params=pltpu.CompilerParams(
            collective_id=2, has_side_effects=True, vmem_limit_bytes=VMEM_LIMIT
        ),
        name="scatter_step",
    )(part, term)


def on_device(n_row, n_col, features, weight, cotangent, tile_values, tile_rows, tile_cols, tile_counts):
    own_rows, width = features.shape
    tiles = own_rows // 128
    sources, values, turned = gather_features(features.T, tile_values[0, 0], n_row)
    sources = sources.reshape(n_row * tiles, width, 128)
    part = tile_pass(turned, tile_rows, tile_cols, tile_counts, sources, n_col * tiles)
    activations, grads, term = node_step(
        part.reshape(n_col, tiles, width, 128), weight, cotangent, n_row, n_col
    )
    grads = grads.reshape(n_col * tiles, width, 128)
    grad_part, activations = tile_pass(
        values, tile_rows, tile_cols, tile_counts, grads, n_row * tiles, activations
    )
    out, weight_grad = scatter_step(grad_part, term, tiles, n_row, n_col)
    return activations, out.T, weight_grad.reshape(weight.shape)


def solution(mesh):
    in_specs = (
        P(("col", "row"), None),
        P(),
        P(("row", "col"), None),
        P("row", "col", None, None, None),
        P("row", "col", None),
        P("row", "col", None),
        P("row", "col"),
    )
    out_specs = (P(("row", "col"), None), P(("col", "row"), None), P())
    return jax.shard_map(
        functools.partial(on_device, mesh.shape["row"], mesh.shape["col"]),
        mesh=mesh,
        in_specs=in_specs,
        out_specs=out_specs,
        check_vma=False,
    )
```

```python
import functools

import jax
import jax.numpy as jnp
from jax import lax
from jax.experimental import pallas as pl
from jax.experimental.pallas import tpu as pltpu
from jax.sharding import PartitionSpec as P

MESH = pl.DeviceIdType.MESH
F32 = jnp.float32
BF16 = jnp.bfloat16
VMEM_LIMIT = 14 * 1024 * 1024
GATHER_VMEM_LIMIT = 20 * 1024 * 1024
PIECES = 4
GROUP = 64
LOADS = 4
TURNS = 8


def inside(chip, chips):
    return (chip >= 0) & (chip < chips)


def dot(a, b, contract_a, contract_b):
    return lax.dot_general(
        a, b, (((contract_a,), (contract_b,)), ((), ())), preferred_element_type=F32
    )


def greet(peers):
    barrier = pltpu.get_barrier_semaphore()
    for peer in peers:
        pl.semaphore_signal(barrier, inc=1, device_id=peer, device_id_type=MESH)
    return lambda: pl.semaphore_wait(barrier, len(peers))


def greet_line(chip, core, chips, peers):
    barrier = pltpu.get_barrier_semaphore()
    for peer in peers:
        pl.semaphore_signal(barrier, inc=1, device_id=peer, device_id_type=MESH)
    count = len(peers)
    for sign in (1, -1):
        there = inside(chip + sign, chips)
        count += there.astype(jnp.int32)

        @pl.when(there)
        def _():
            pl.semaphore_signal(
                barrier, inc=1, device_id={"row": (chip + sign) * 2 + core}, device_id_type=MESH
            )

    return lambda: pl.semaphore_wait(barrier, count)


def remote(src, dst, send_sem, recv_sem, peer):
    return pltpu.make_async_remote_copy(
        src_ref=src,
        dst_ref=dst,
        send_sem=send_sem,
        recv_sem=recv_sem,
        device_id=peer,
        device_id_type=MESH,
    )


def gather_kernel(n_row, f_ref, values_ref, out_ref, kept_ref, turned_ref, load_sem, l_send, l_recv, p_send, p_recv):
    chips = n_row // 2
    me = lax.axis_index("row")
    chip, core = me // 2, me % 2
    partner = {"row": chip * 2 + 1 - core}
    tiles = out_ref.shape[1]
    half = tiles // PIECES
    slots = kept_ref.shape[0]
    loads = []
    for i in range(LOADS):
        part = pl.ds(i * (slots // LOADS), slots // LOADS)
        loads.append(pltpu.make_async_copy(values_ref.at[part], kept_ref.at[part], load_sem.at[i]))
    ready = greet_line(chip, core, chips, [partner])
    for load in loads:
        load.start()
    for t in range(tiles):
        out_ref[me, t] = f_ref[:, t * 128 : (t + 1) * 128]
    ready()

    def block(source, q):
        return out_ref.at[source, pl.ds(q * half, half)]

    def lane(side, hop, q, source, sign):
        piece = block(source, q)
        return remote(
            piece, piece, l_send.at[side, hop - 1, q], l_recv.at[side, hop - 1, q],
            {"row": me + 2 * sign},
        )

    def across(side, hop, q, source):
        piece = block(source, q)
        return remote(piece, piece, p_send.at[side, hop, q], p_recv.at[side, hop, q], partner)

    sides = ((0, 1), (1, -1))
    for q in range(PIECES):
        for side, sign in sides:
            @pl.when(inside(chip + sign, chips))
            def _():
                lane(side, 1, q, me, sign).start()
        across(0, 0, q, me).start()
    def turn(i, carry):
        for u in range(TURNS):
            turned_ref[i * TURNS + u] = kept_ref[i * TURNS + u].T
        return carry

    waited = 0
    rounds = (chips - 1) * PIECES
    for hop in range(1, chips):
        for q in range(PIECES):
            now = (hop - 1) * PIECES + q
            first, last = (slots // TURNS * n // rounds for n in (now, now + 1))
            while waited < LOADS and waited * (slots // LOADS) < last * TURNS:
                loads[waited].wait()
                waited += 1
            lax.fori_loop(first, last, turn, 0)
            for side, sign in sides:
                source = me - 2 * sign * hop
                came = inside(chip - sign * hop, chips)

                @pl.when(came)
                def _():
                    lane(side, hop, q, source, sign).wait_recv()

                if hop + 1 < chips:
                    @pl.when(came & inside(chip + sign, chips))
                    def _():
                        lane(side, hop + 1, q, source, sign).start()

                @pl.when(came)
                def _():
                    across(side, hop, q, source).start()
    for q in range(PIECES):
        across(0, 0, q, chip * 2 + 1 - core).wait_recv()
        across(0, 0, q, me).wait_send()
        for side, sign in sides:
            @pl.when(inside(chip + sign, chips))
            def _():
                lane(side, 1, q, me, sign).wait_send()
    for hop in range(1, chips):
        for q in range(PIECES):
            for side, sign in sides:
                source = me - 2 * sign * hop
                came = inside(chip - sign * hop, chips)

                @pl.when(came)
                def _():
                    across(side, hop, q, (chip - sign * hop) * 2 + 1 - core).wait_recv()
                    across(side, hop, q, source).wait_send()

                if hop + 1 < chips:
                    @pl.when(came & inside(chip + sign, chips))
                    def _():
                        lane(side, hop + 1, q, source, sign).wait_send()


def gather_features(features, values, n_row):
    width, rows = features.shape
    tiles = rows // 128
    chips = n_row // 2
    vmem = pl.BlockSpec(memory_space=pltpu.VMEM)
    dma = pltpu.SemaphoreType.DMA
    return pl.pallas_call(
        functools.partial(gather_kernel, n_row),
        out_shape=(
            jax.ShapeDtypeStruct((n_row, tiles, width, 128), BF16),
            jax.ShapeDtypeStruct(values.shape, BF16),
            jax.ShapeDtypeStruct(values.shape, BF16),
        ),
        in_specs=[vmem, pl.BlockSpec(memory_space=pl.ANY)],
        out_specs=(vmem, vmem, vmem),
        scratch_shapes=[
            dma((LOADS,)),
            dma((2, chips - 1, PIECES)),
            dma((2, chips - 1, PIECES)),
            dma((2, chips, PIECES)),
            dma((2, chips, PIECES)),
        ],
        compiler_params=pltpu.CompilerParams(
            collective_id=0, has_side_effects=True, vmem_limit_bytes=GATHER_VMEM_LIMIT
        ),
        name="gather_features",
    )(features, values)


def add_tiles(live_ref, targets_ref, picks_ref, values_ref, source_ref, even, odd):
    group = GROUP
    live = live_ref[0, 0]
    spare = even.shape[0] - 1
    even[...] = jnp.zeros_like(even)
    odd[...] = jnp.zeros_like(odd)

    def body(g, carry):
        for u in range(group):
            slot = g * group + u
            pick = picks_ref[0, 0, slot]
            target = jnp.where(slot < live, targets_ref[0, 0, slot], spare)
            product = dot(source_ref[pick], values_ref[slot], 1, 0)
            acc = odd if u % 2 else even
            acc[target] += product
        return carry

    groups = (live + group - 1) // group
    lax.fori_loop(0, groups, body, 0)


def forward_kernel(live_ref, rows_ref, cols_ref, values_ref, source_ref, out_ref, even, odd):
    add_tiles(live_ref, rows_ref, cols_ref, values_ref, source_ref, even, odd)
    n = out_ref.shape[0]
    out_ref[...] = (even[0:n] + odd[0:n]).astype(BF16)


def backward_kernel(
    live_ref, rows_ref, cols_ref, values_ref, source_ref, act_ref, out_ref, act_out_ref, even, odd, sem
):
    write = pltpu.make_async_copy(act_ref, act_out_ref, sem)
    write.start()
    add_tiles(live_ref, cols_ref, rows_ref, values_ref, source_ref, even, odd)
    n = out_ref.shape[0]
    out_ref[...] = even[0:n] + odd[0:n]
    write.wait()


def tile_pass(values, rows, cols, live, source, n_targets, activations=None):
    slots, side, _ = values.shape
    width = source.shape[1]
    smem = pl.BlockSpec(memory_space=pltpu.SMEM)
    vmem = pl.BlockSpec(memory_space=pltpu.VMEM)
    cost = pl.CostEstimate(
        flops=2 * slots * side * side * width,
        bytes_accessed=2 * slots * side * side,
        transcendentals=0,
    )
    params = pltpu.CompilerParams(vmem_limit_bytes=VMEM_LIMIT)
    totals = [pltpu.VMEM((n_targets + 1, width, side), F32)] * 2
    if activations is None:
        return pl.pallas_call(
            forward_kernel,
            out_shape=jax.ShapeDtypeStruct((n_targets, width, side), BF16),
            in_specs=[smem, smem, smem, vmem, vmem],
            out_specs=vmem,
            scratch_shapes=totals,
            compiler_params=params,
            cost_estimate=cost,
            name="tiles_forward",
        )(live, rows, cols, values, source)
    return pl.pallas_call(
        backward_kernel,
        out_shape=(
            jax.ShapeDtypeStruct((n_targets, width, side), F32),
            jax.ShapeDtypeStruct(activations.shape, BF16),
        ),
        in_specs=[smem, smem, smem, vmem, vmem, vmem],
        out_specs=(vmem, pl.BlockSpec(memory_space=pl.ANY)),
        scratch_shapes=totals + [pltpu.SemaphoreType.DMA],
        compiler_params=params,
        cost_estimate=cost,
        name="tiles_backward",
    )(live, rows, cols, values, source, activations)


def node_kernel(
    n_row, n_col,
    part_ref, weight_ref, cot_ref,
    act_ref, grads_ref, wgrad_ref,
    came, a_send, a_recv, g_send, g_recv,
):
    col = lax.axis_index("col")
    across = [{"col": lax.rem(col + d, n_col)} for d in range(1, n_col)]
    ready = greet(across)
    ready()
    tiles = part_ref.shape[1]
    half = tiles // PIECES
    copies = []
    arrivals = []
    for q in range(PIECES):
        piece = pl.ds(q * half, half)
        for d in range(1, n_col):
            copy = remote(
                part_ref.at[lax.rem(col + d, n_col), piece], came.at[d - 1, piece],
                a_send.at[d - 1, q], a_recv.at[d - 1, q], across[d - 1],
            )
            copy.start()
            copies.append(copy)
            arrivals.append(copy)
    square = n_col == 4
    beside = col + 1 - 2 * lax.rem(col, 2)
    above = lax.rem(col + 2, n_col)
    opposite = lax.rem(beside + 2, n_col)

    def grads_copy(k, q, source, target):
        block = grads_ref.at[source, pl.ds(q * half, half)]
        return remote(block, block, g_send.at[k, q], g_recv.at[k, q], {"col": target})

    def send_grads(k, q, source, target):
        copy = grads_copy(k, q, source, target)
        copy.start()
        copies.append(copy)

    def relay(q):
        grads_copy(0, q, beside, beside).wait_recv()
        grads_copy(1, q, above, above).wait_recv()
        if q % 2 == 0:
            send_grads(2, q, beside, above)
        else:
            send_grads(2, q, above, beside)

    weight = weight_ref[...]
    total = None
    for q in range(PIECES):
        for copy in arrivals[q * (n_col - 1) : (q + 1) * (n_col - 1)]:
            copy.wait_recv()
        for t in range(q * half, (q + 1) * half):
            agg = part_ref[col, t].astype(F32)
            for d in range(1, n_col):
                agg += came[d - 1, t].astype(F32)
            low = agg.astype(BF16)
            nodes = slice(t * 128, (t + 1) * 128)
            pre = jnp.dot(agg.T.astype(BF16), weight, preferred_element_type=F32)
            sigma = 1.0 / (1.0 + jnp.exp(-pre))
            act_ref[nodes, :] = (pre * sigma).astype(BF16)
            cot = cot_ref[nodes, :].astype(F32)
            pre_grad = (cot * sigma * (1.0 + pre * (1.0 - sigma))).astype(BF16)
            grads_ref[col, t] = dot(weight, pre_grad, 1, 1).astype(BF16)
            term = jnp.dot(low, pre_grad, preferred_element_type=F32)
            total = term if total is None else total + term
        if square:
            send_grads(0, q, col, beside)
            send_grads(1, q, col, above)
            if q >= 2:
                relay(q - 2)
        else:
            for d in range(1, n_col):
                send_grads(d - 1, q, col, lax.rem(col + d, n_col))
    depth = wgrad_ref.shape[1]
    for r in range(n_row):
        wgrad_ref[r] = total[r * depth : (r + 1) * depth]
    if square:
        for q in range(max(0, PIECES - 2), PIECES):
            relay(q)
    for q in range(PIECES):
        if square:
            grads_copy(2, q, opposite, above).wait_recv()
        else:
            for d in range(1, n_col):
                source = lax.rem(col + n_col - d, n_col)
                grads_copy(d - 1, q, source, source).wait_recv()
    for copy in copies:
        copy.wait_send()


def node_step(part, weight, cotangent, n_row, n_col):
    _, tiles, width, side = part.shape
    hidden = weight.shape[1]
    depth = width // n_row
    vmem = pl.BlockSpec(memory_space=pltpu.VMEM)
    dma = pltpu.SemaphoreType.DMA
    return pl.pallas_call(
        functools.partial(node_kernel, n_row, n_col),
        out_shape=(
            jax.ShapeDtypeStruct(cotangent.shape, BF16),
            jax.ShapeDtypeStruct(part.shape, BF16),
            jax.ShapeDtypeStruct((n_row, depth, hidden), F32),
        ),
        in_specs=[vmem, vmem, vmem],
        out_specs=(vmem, vmem, vmem),
        scratch_shapes=[
            pltpu.VMEM((n_col - 1, tiles, width, side), BF16),
            dma((n_col - 1, PIECES)),
            dma((n_col - 1, PIECES)),
            dma((n_col - 1, PIECES)),
            dma((n_col - 1, PIECES)),
        ],
        compiler_params=pltpu.CompilerParams(
            collective_id=1, has_side_effects=True, vmem_limit_bytes=VMEM_LIMIT
        ),
        name="node_step",
    )(part, weight, cotangent)


def scatter_kernel(
    n_row, n_col,
    part_ref, term_ref,
    out_ref, wgrad_ref,
    other, leaving, came, total_ref, wrows, wcols, wsum,
    p_send, p_recv, l_send, l_recv, r_send, r_recv, c_send, c_recv, w_send, w_recv,
):
    chips = n_row // 2
    row, col = lax.axis_index("row"), lax.axis_index("col")
    chip, core = row // 2, row % 2
    partner = {"row": chip * 2 + 1 - core}
    along = [lax.rem(row + d, n_row) for d in range(1, n_row)]
    across = [{"col": lax.rem(col + d, n_col)} for d in range(1, n_col)]
    ready = greet([{"row": r} for r in along] + across)
    ready()
    tiles = came.shape[2]
    half = tiles // PIECES
    sides = ((0, 1), (1, -1))
    order = [(side, sign, hop) for hop in range(chips - 1, 0, -1) for side, sign in sides]

    def pair(side, hop, q, to_chip):
        piece = pl.ds(q * half, half)
        first = (to_chip * 2 + 1 - core) * tiles + q * half
        return remote(
            part_ref.at[pl.ds(first, half)], other.at[side, hop, piece],
            p_send.at[side, hop, q], p_recv.at[side, hop, q], partner,
        )

    def lane(side, hop, q, sign):
        piece = pl.ds(q * half, half)
        return remote(
            leaving.at[side, hop - 1, piece], came.at[side, hop - 1, piece],
            l_send.at[side, hop - 1, q], l_recv.at[side, hop - 1, q],
            {"row": row + 2 * sign},
        )

    for side, sign, hop in order:
        @pl.when(inside(chip + sign * hop, chips))
        def _():
            for q in range(PIECES):
                pair(side, hop, q, chip + sign * hop).start()
    for q in range(PIECES):
        pair(0, 0, q, chip).start()
    copies = []
    arrivals = []
    for d in range(1, n_row):
        copy = remote(
            term_ref.at[along[d - 1]], wrows.at[d - 1], r_send.at[d - 1], r_recv.at[d - 1],
            {"row": along[d - 1]},
        )
        copy.start()
        copies.append(copy)
        arrivals.append(copy)

    def sum_rows():
        for copy in arrivals:
            copy.wait_recv()
        total = term_ref[row]
        for d in range(1, n_row):
            total += wrows[d - 1]
        wcols[col] = total
        for d in range(1, n_col):
            mine = wcols.at[col]
            copy = remote(mine, mine, c_send.at[d - 1], c_recv.at[d - 1], across[d - 1])
            copy.start()
            copies.append(copy)

    def sum_cols():
        for d in range(1, n_col):
            theirs = wcols.at[lax.rem(col + n_col - d, n_col)]
            remote(theirs, theirs, c_send.at[d - 1], c_recv.at[d - 1], across[d - 1]).wait_recv()
        total = wcols[0]
        for c in range(1, n_col):
            total += wcols[c]
        wsum[...] = total
        wgrad_ref[row] = total
        for d in range(1, n_row):
            copy = remote(wsum, wgrad_ref.at[row], w_send.at[d - 1], w_recv.at[d - 1], {"row": along[d - 1]})
            copy.start()
            copies.append(copy)

    for hop in range(chips - 1, 0, -1):
        for q in range(PIECES):
            for side, sign in sides:
                to_chip = chip + sign * hop
                goes = inside(to_chip, chips)

                @pl.when(goes)
                def _():
                    pair(side, hop, q, to_chip).wait_recv()
                    for t in range(q * half, (q + 1) * half):
                        total_ref[t] = part_ref[(to_chip * 2 + core) * tiles + t] + other[side, hop, t]

                if hop + 1 < chips:
                    @pl.when(goes & inside(chip - sign, chips))
                    def _():
                        lane(side, hop + 1, q, sign).wait_recv()
                        for t in range(q * half, (q + 1) * half):
                            total_ref[t] = total_ref[t] + came[side, hop, t].astype(F32)

                @pl.when(goes)
                def _():
                    for t in range(q * half, (q + 1) * half):
                        leaving[side, hop - 1, t] = total_ref[t].astype(BF16)
                    lane(side, hop, q, sign).start()
        if hop == chips - 1:
            sum_rows()
        if hop == max(1, chips - 2):
            sum_cols()
    for q in range(PIECES):
        pair(0, 0, q, chip).wait_recv()
        for t in range(q * half, (q + 1) * half):
            total_ref[t] = part_ref[row * tiles + t] + other[0, 0, t]
        for side, sign in sides:
            @pl.when(inside(chip - sign, chips))
            def _():
                lane(side, 1, q, sign).wait_recv()
                for t in range(q * half, (q + 1) * half):
                    total_ref[t] = total_ref[t] + came[side, 0, t].astype(F32)
        for t in range(q * half, (q + 1) * half):
            out_ref[:, t * 128 : (t + 1) * 128] = total_ref[t].astype(BF16)
    for d in range(1, n_row):
        source = lax.rem(row + n_row - d, n_row)
        remote(wsum, wgrad_ref.at[source], w_send.at[d - 1], w_recv.at[d - 1], partner).wait_recv()
    for copy in copies:
        copy.wait_send()
    for q in range(PIECES):
        pair(0, 0, q, chip).wait_send()
        for side, sign, hop in order:
            @pl.when(inside(chip + sign * hop, chips))
            def _():
                pair(side, hop, q, chip + sign * hop).wait_send()
                lane(side, hop, q, sign).wait_send()


def scatter_step(part, term, tiles, n_row, n_col):
    _, width, side = part.shape
    _, depth, hidden = term.shape
    chips = n_row // 2
    vmem = pl.BlockSpec(memory_space=pltpu.VMEM)
    dma = pltpu.SemaphoreType.DMA
    return pl.pallas_call(
        functools.partial(scatter_kernel, n_row, n_col),
        out_shape=(
            jax.ShapeDtypeStruct((width, tiles * side), BF16),
            jax.ShapeDtypeStruct((n_row, depth, hidden), F32),
        ),
        in_specs=[vmem, vmem],
        out_specs=(vmem, vmem),
        scratch_shapes=[
            pltpu.VMEM((2, chips, tiles, width, side), F32),
            pltpu.VMEM((2, chips - 1, tiles, width, side), BF16),
            pltpu.VMEM((2, chips - 1, tiles, width, side), BF16),
            pltpu.VMEM((tiles, width, side), F32),
            pltpu.VMEM((n_row - 1, depth, hidden), F32),
            pltpu.VMEM((n_col, depth, hidden), F32),
            pltpu.VMEM((depth, hidden), F32),
            dma((2, chips, PIECES)),
            dma((2, chips, PIECES)),
            dma((2, chips - 1, PIECES)),
            dma((2, chips - 1, PIECES)),
            dma((n_row - 1,)),
            dma((n_row - 1,)),
            dma((n_col - 1,)),
            dma((n_col - 1,)),
            dma((n_row - 1,)),
            dma((n_row - 1,)),
        ],
        compiler_params=pltpu.CompilerParams(
            collective_id=2, has_side_effects=True, vmem_limit_bytes=VMEM_LIMIT
        ),
        name="scatter_step",
    )(part, term)


def on_device(n_row, n_col, features, weight, cotangent, tile_values, tile_rows, tile_cols, tile_counts):
    own_rows, width = features.shape
    tiles = own_rows // 128
    sources, values, turned = gather_features(features.T, tile_values[0, 0], n_row)
    sources = sources.reshape(n_row * tiles, width, 128)
    part = tile_pass(turned, tile_rows, tile_cols, tile_counts, sources, n_col * tiles)
    activations, grads, term = node_step(
        part.reshape(n_col, tiles, width, 128), weight, cotangent, n_row, n_col
    )
    grads = grads.reshape(n_col * tiles, width, 128)
    grad_part, activations = tile_pass(
        values, tile_rows, tile_cols, tile_counts, grads, n_row * tiles, activations
    )
    out, weight_grad = scatter_step(grad_part, term, tiles, n_row, n_col)
    return activations, out.T, weight_grad.reshape(weight.shape)


def solution(mesh):
    in_specs = (
        P(("col", "row"), None),
        P(),
        P(("row", "col"), None),
        P("row", "col", None, None, None),
        P("row", "col", None),
        P("row", "col", None),
        P("row", "col"),
    )
    out_specs = (P(("row", "col"), None), P(("col", "row"), None), P())
    return jax.shard_map(
        functools.partial(on_device, mesh.shape["row"], mesh.shape["col"]),
        mesh=mesh,
        in_specs=in_specs,
        out_specs=out_specs,
        check_vma=False,
    )
```

```python
import functools

import jax
import jax.numpy as jnp
from jax import lax
from jax.experimental import pallas as pl
from jax.experimental.pallas import tpu as pltpu
from jax.sharding import PartitionSpec as P

MESH = pl.DeviceIdType.MESH
F32 = jnp.float32
BF16 = jnp.bfloat16
VMEM_LIMIT = 14 * 1024 * 1024
GATHER_VMEM_LIMIT = 20 * 1024 * 1024
PIECES = 4
GROUP = 96
LOADS = 4
TURNS = 16


def inside(chip, chips):
    return (chip >= 0) & (chip < chips)


def dot(a, b, contract_a, contract_b):
    return lax.dot_general(
        a, b, (((contract_a,), (contract_b,)), ((), ())), preferred_element_type=F32
    )


def greet(peers):
    barrier = pltpu.get_barrier_semaphore()
    for peer in peers:
        pl.semaphore_signal(barrier, inc=1, device_id=peer, device_id_type=MESH)
    return lambda: pl.semaphore_wait(barrier, len(peers))


def greet_line(chip, core, chips, peers):
    barrier = pltpu.get_barrier_semaphore()
    for peer in peers:
        pl.semaphore_signal(barrier, inc=1, device_id=peer, device_id_type=MESH)
    count = len(peers)
    for sign in (1, -1):
        there = inside(chip + sign, chips)
        count += there.astype(jnp.int32)

        @pl.when(there)
        def _():
            pl.semaphore_signal(
                barrier, inc=1, device_id={"row": (chip + sign) * 2 + core}, device_id_type=MESH
            )

    return lambda: pl.semaphore_wait(barrier, count)


def remote(src, dst, send_sem, recv_sem, peer):
    return pltpu.make_async_remote_copy(
        src_ref=src,
        dst_ref=dst,
        send_sem=send_sem,
        recv_sem=recv_sem,
        device_id=peer,
        device_id_type=MESH,
    )


def gather_kernel(n_row, f_ref, values_ref, out_ref, kept_ref, turned_ref, load_sem, l_send, l_recv, p_send, p_recv):
    chips = n_row // 2
    me = lax.axis_index("row")
    chip, core = me // 2, me % 2
    partner = {"row": chip * 2 + 1 - core}
    tiles = out_ref.shape[1]
    half = tiles // PIECES
    slots = kept_ref.shape[0]
    loads = []
    for i in range(LOADS):
        part = pl.ds(i * (slots // LOADS), slots // LOADS)
        loads.append(pltpu.make_async_copy(values_ref.at[part], kept_ref.at[part], load_sem.at[i]))
    ready = greet_line(chip, core, chips, [partner])
    for load in loads:
        load.start()
    for t in range(tiles):
        out_ref[me, t] = f_ref[:, t * 128 : (t + 1) * 128]
    ready()

    def block(source, q):
        return out_ref.at[source, pl.ds(q * half, half)]

    def lane(side, hop, q, source, sign):
        piece = block(source, q)
        return remote(
            piece, piece, l_send.at[side, hop - 1, q], l_recv.at[side, hop - 1, q],
            {"row": me + 2 * sign},
        )

    def across(side, hop, q, source):
        piece = block(source, q)
        return remote(piece, piece, p_send.at[side, hop, q], p_recv.at[side, hop, q], partner)

    sides = ((0, 1), (1, -1))
    for q in range(PIECES):
        for side, sign in sides:
            @pl.when(inside(chip + sign, chips))
            def _():
                lane(side, 1, q, me, sign).start()
        across(0, 0, q, me).start()
    def turn(i, carry):
        for u in range(TURNS):
            turned_ref[i * TURNS + u] = kept_ref[i * TURNS + u].T
        return carry

    waited = 0
    rounds = (chips - 1) * PIECES
    for hop in range(1, chips):
        for q in range(PIECES):
            now = (hop - 1) * PIECES + q
            first, last = (slots // TURNS * n // rounds for n in (now, now + 1))
            while waited < LOADS and waited * (slots // LOADS) < last * TURNS:
                loads[waited].wait()
                waited += 1
            lax.fori_loop(first, last, turn, 0)
            for side, sign in sides:
                source = me - 2 * sign * hop
                came = inside(chip - sign * hop, chips)

                @pl.when(came)
                def _():
                    lane(side, hop, q, source, sign).wait_recv()

                if hop + 1 < chips:
                    @pl.when(came & inside(chip + sign, chips))
                    def _():
                        lane(side, hop + 1, q, source, sign).start()

                @pl.when(came)
                def _():
                    across(side, hop, q, source).start()
    for q in range(PIECES):
        across(0, 0, q, chip * 2 + 1 - core).wait_recv()
        across(0, 0, q, me).wait_send()
        for side, sign in sides:
            @pl.when(inside(chip + sign, chips))
            def _():
                lane(side, 1, q, me, sign).wait_send()
    for hop in range(1, chips):
        for q in range(PIECES):
            for side, sign in sides:
                source = me - 2 * sign * hop
                came = inside(chip - sign * hop, chips)

                @pl.when(came)
                def _():
                    across(side, hop, q, (chip - sign * hop) * 2 + 1 - core).wait_recv()
                    across(side, hop, q, source).wait_send()

                if hop + 1 < chips:
                    @pl.when(came & inside(chip + sign, chips))
                    def _():
                        lane(side, hop + 1, q, source, sign).wait_send()


def gather_features(features, values, n_row):
    width, rows = features.shape
    tiles = rows // 128
    chips = n_row // 2
    vmem = pl.BlockSpec(memory_space=pltpu.VMEM)
    dma = pltpu.SemaphoreType.DMA
    return pl.pallas_call(
        functools.partial(gather_kernel, n_row),
        out_shape=(
            jax.ShapeDtypeStruct((n_row, tiles, width, 128), BF16),
            jax.ShapeDtypeStruct(values.shape, BF16),
            jax.ShapeDtypeStruct(values.shape, BF16),
        ),
        in_specs=[vmem, pl.BlockSpec(memory_space=pl.ANY)],
        out_specs=(vmem, vmem, vmem),
        scratch_shapes=[
            dma((LOADS,)),
            dma((2, chips - 1, PIECES)),
            dma((2, chips - 1, PIECES)),
            dma((2, chips, PIECES)),
            dma((2, chips, PIECES)),
        ],
        compiler_params=pltpu.CompilerParams(
            collective_id=0, has_side_effects=True, vmem_limit_bytes=GATHER_VMEM_LIMIT
        ),
        name="gather_features",
    )(features, values)


def add_tiles(live_ref, targets_ref, picks_ref, values_ref, source_ref, even, odd):
    group = GROUP
    live = live_ref[0, 0]
    spare = even.shape[0] - 1
    even[...] = jnp.zeros_like(even)
    odd[...] = jnp.zeros_like(odd)

    def body(g, carry):
        for u in range(group):
            slot = g * group + u
            pick = picks_ref[0, 0, slot]
            target = jnp.where(slot < live, targets_ref[0, 0, slot], spare)
            product = dot(source_ref[pick], values_ref[slot], 1, 0)
            acc = odd if u % 2 else even
            acc[target] += product
        return carry

    groups = (live + group - 1) // group
    lax.fori_loop(0, groups, body, 0)


def forward_kernel(live_ref, rows_ref, cols_ref, values_ref, source_ref, out_ref, even, odd):
    add_tiles(live_ref, rows_ref, cols_ref, values_ref, source_ref, even, odd)
    n = out_ref.shape[0]
    out_ref[...] = (even[0:n] + odd[0:n]).astype(BF16)


def backward_kernel(
    live_ref, rows_ref, cols_ref, values_ref, source_ref, act_ref, out_ref, act_out_ref, even, odd, sem
):
    write = pltpu.make_async_copy(act_ref, act_out_ref, sem)
    write.start()
    add_tiles(live_ref, cols_ref, rows_ref, values_ref, source_ref, even, odd)
    n = out_ref.shape[0]
    out_ref[...] = even[0:n] + odd[0:n]
    write.wait()


def tile_pass(values, rows, cols, live, source, n_targets, activations=None):
    slots, side, _ = values.shape
    width = source.shape[1]
    smem = pl.BlockSpec(memory_space=pltpu.SMEM)
    vmem = pl.BlockSpec(memory_space=pltpu.VMEM)
    cost = pl.CostEstimate(
        flops=2 * slots * side * side * width,
        bytes_accessed=2 * slots * side * side,
        transcendentals=0,
    )
    params = pltpu.CompilerParams(vmem_limit_bytes=VMEM_LIMIT)
    totals = [pltpu.VMEM((n_targets + 1, width, side), F32)] * 2
    if activations is None:
        return pl.pallas_call(
            forward_kernel,
            out_shape=jax.ShapeDtypeStruct((n_targets, width, side), BF16),
            in_specs=[smem, smem, smem, vmem, vmem],
            out_specs=vmem,
            scratch_shapes=totals,
            compiler_params=params,
            cost_estimate=cost,
            name="tiles_forward",
        )(live, rows, cols, values, source)
    return pl.pallas_call(
        backward_kernel,
        out_shape=(
            jax.ShapeDtypeStruct((n_targets, width, side), F32),
            jax.ShapeDtypeStruct(activations.shape, BF16),
        ),
        in_specs=[smem, smem, smem, vmem, vmem, vmem],
        out_specs=(vmem, pl.BlockSpec(memory_space=pl.ANY)),
        scratch_shapes=totals + [pltpu.SemaphoreType.DMA],
        compiler_params=params,
        cost_estimate=cost,
        name="tiles_backward",
    )(live, rows, cols, values, source, activations)


def node_kernel(
    n_row, n_col,
    part_ref, weight_ref, cot_ref,
    act_ref, grads_ref, wgrad_ref,
    came, a_send, a_recv, g_send, g_recv,
):
    col = lax.axis_index("col")
    across = [{"col": lax.rem(col + d, n_col)} for d in range(1, n_col)]
    ready = greet(across)
    ready()
    tiles = part_ref.shape[1]
    half = tiles // PIECES
    copies = []
    arrivals = []
    for q in range(PIECES):
        piece = pl.ds(q * half, half)
        for d in range(1, n_col):
            copy = remote(
                part_ref.at[lax.rem(col + d, n_col), piece], came.at[d - 1, piece],
                a_send.at[d - 1, q], a_recv.at[d - 1, q], across[d - 1],
            )
            copy.start()
            copies.append(copy)
            arrivals.append(copy)
    def grads_copy(k, q, source, target):
        block = grads_ref.at[source, pl.ds(q * half, half)]
        return remote(block, block, g_send.at[k, q], g_recv.at[k, q], {"col": target})

    weight = weight_ref[...]
    total = None
    for q in range(PIECES):
        for copy in arrivals[q * (n_col - 1) : (q + 1) * (n_col - 1)]:
            copy.wait_recv()
        for t in range(q * half, (q + 1) * half):
            agg = part_ref[col, t].astype(F32)
            for d in range(1, n_col):
                agg += came[d - 1, t].astype(F32)
            low = agg.astype(BF16)
            nodes = slice(t * 128, (t + 1) * 128)
            pre = jnp.dot(agg.T.astype(BF16), weight, preferred_element_type=F32)
            sigma = 1.0 / (1.0 + jnp.exp(-pre))
            act_ref[nodes, :] = (pre * sigma).astype(BF16)
            cot = cot_ref[nodes, :].astype(F32)
            pre_grad = (cot * sigma * (1.0 + pre * (1.0 - sigma))).astype(BF16)
            grads_ref[col, t] = dot(weight, pre_grad, 1, 1).astype(BF16)
            term = jnp.dot(low, pre_grad, preferred_element_type=F32)
            total = term if total is None else total + term
        for d in range(1, n_col):
            copy = grads_copy(d - 1, q, col, lax.rem(col + d, n_col))
            copy.start()
            copies.append(copy)
    depth = wgrad_ref.shape[1]
    for r in range(n_row):
        wgrad_ref[r] = total[r * depth : (r + 1) * depth]
    for q in range(PIECES):
        for d in range(1, n_col):
            source = lax.rem(col + n_col - d, n_col)
            grads_copy(d - 1, q, source, source).wait_recv()
    for copy in copies:
        copy.wait_send()


def node_step(part, weight, cotangent, n_row, n_col):
    _, tiles, width, side = part.shape
    hidden = weight.shape[1]
    depth = width // n_row
    vmem = pl.BlockSpec(memory_space=pltpu.VMEM)
    dma = pltpu.SemaphoreType.DMA
    return pl.pallas_call(
        functools.partial(node_kernel, n_row, n_col),
        out_shape=(
            jax.ShapeDtypeStruct(cotangent.shape, BF16),
            jax.ShapeDtypeStruct(part.shape, BF16),
            jax.ShapeDtypeStruct((n_row, depth, hidden), F32),
        ),
        in_specs=[vmem, vmem, vmem],
        out_specs=(vmem, vmem, vmem),
        scratch_shapes=[
            pltpu.VMEM((n_col - 1, tiles, width, side), BF16),
            dma((n_col - 1, PIECES)),
            dma((n_col - 1, PIECES)),
            dma((n_col - 1, PIECES)),
            dma((n_col - 1, PIECES)),
        ],
        compiler_params=pltpu.CompilerParams(
            collective_id=1, has_side_effects=True, vmem_limit_bytes=VMEM_LIMIT
        ),
        name="node_step",
    )(part, weight, cotangent)


def scatter_kernel(
    n_row, n_col,
    part_ref, term_ref,
    out_ref, wgrad_ref,
    other, leaving, came, total_ref, wrows, wcols, wsum,
    p_send, p_recv, l_send, l_recv, r_send, r_recv, c_send, c_recv, w_send, w_recv,
):
    chips = n_row // 2
    row, col = lax.axis_index("row"), lax.axis_index("col")
    chip, core = row // 2, row % 2
    partner = {"row": chip * 2 + 1 - core}
    along = [lax.rem(row + d, n_row) for d in range(1, n_row)]
    across = [{"col": lax.rem(col + d, n_col)} for d in range(1, n_col)]
    ready = greet([{"row": r} for r in along] + across)
    ready()
    tiles = came.shape[2]
    half = tiles // PIECES
    sides = ((0, 1), (1, -1))
    order = [(side, sign, hop) for hop in range(chips - 1, 0, -1) for side, sign in sides]

    def pair(side, hop, q, to_chip):
        piece = pl.ds(q * half, half)
        first = (to_chip * 2 + 1 - core) * tiles + q * half
        return remote(
            part_ref.at[pl.ds(first, half)], other.at[side, hop, piece],
            p_send.at[side, hop, q], p_recv.at[side, hop, q], partner,
        )

    def lane(side, hop, q, sign):
        piece = pl.ds(q * half, half)
        return remote(
            leaving.at[side, hop - 1, piece], came.at[side, hop - 1, piece],
            l_send.at[side, hop - 1, q], l_recv.at[side, hop - 1, q],
            {"row": row + 2 * sign},
        )

    for side, sign, hop in order:
        @pl.when(inside(chip + sign * hop, chips))
        def _():
            for q in range(PIECES):
                pair(side, hop, q, chip + sign * hop).start()
    for q in range(PIECES):
        pair(0, 0, q, chip).start()
    copies = []
    arrivals = []
    for d in range(1, n_row):
        copy = remote(
            term_ref.at[along[d - 1]], wrows.at[d - 1], r_send.at[d - 1], r_recv.at[d - 1],
            {"row": along[d - 1]},
        )
        copy.start()
        copies.append(copy)
        arrivals.append(copy)

    def sum_rows():
        for copy in arrivals:
            copy.wait_recv()
        total = term_ref[row]
        for d in range(1, n_row):
            total += wrows[d - 1]
        wcols[col] = total
        for d in range(1, n_col):
            mine = wcols.at[col]
            copy = remote(mine, mine, c_send.at[d - 1], c_recv.at[d - 1], across[d - 1])
            copy.start()
            copies.append(copy)

    def sum_cols():
        for d in range(1, n_col):
            theirs = wcols.at[lax.rem(col + n_col - d, n_col)]
            remote(theirs, theirs, c_send.at[d - 1], c_recv.at[d - 1], across[d - 1]).wait_recv()
        total = wcols[0]
        for c in range(1, n_col):
            total += wcols[c]
        wsum[...] = total
        wgrad_ref[row] = total
        for d in range(1, n_row):
            copy = remote(wsum, wgrad_ref.at[row], w_send.at[d - 1], w_recv.at[d - 1], {"row": along[d - 1]})
            copy.start()
            copies.append(copy)

    for hop in range(chips - 1, 0, -1):
        for q in range(PIECES):
            for side, sign in sides:
                to_chip = chip + sign * hop
                goes = inside(to_chip, chips)

                @pl.when(goes)
                def _():
                    pair(side, hop, q, to_chip).wait_recv()
                    for t in range(q * half, (q + 1) * half):
                        total_ref[t] = part_ref[(to_chip * 2 + core) * tiles + t] + other[side, hop, t]

                if hop + 1 < chips:
                    @pl.when(goes & inside(chip - sign, chips))
                    def _():
                        lane(side, hop + 1, q, sign).wait_recv()
                        for t in range(q * half, (q + 1) * half):
                            total_ref[t] = total_ref[t] + came[side, hop, t].astype(F32)

                @pl.when(goes)
                def _():
                    for t in range(q * half, (q + 1) * half):
                        leaving[side, hop - 1, t] = total_ref[t].astype(BF16)
                    lane(side, hop, q, sign).start()
        if hop == chips - 1:
            sum_rows()
        if hop == max(1, chips - 2):
            sum_cols()
    for q in range(PIECES):
        pair(0, 0, q, chip).wait_recv()
        for t in range(q * half, (q + 1) * half):
            total_ref[t] = part_ref[row * tiles + t] + other[0, 0, t]
        for side, sign in sides:
            @pl.when(inside(chip - sign, chips))
            def _():
                lane(side, 1, q, sign).wait_recv()
                for t in range(q * half, (q + 1) * half):
                    total_ref[t] = total_ref[t] + came[side, 0, t].astype(F32)
        for t in range(q * half, (q + 1) * half):
            out_ref[:, t * 128 : (t + 1) * 128] = total_ref[t].astype(BF16)
    for d in range(1, n_row):
        source = lax.rem(row + n_row - d, n_row)
        remote(wsum, wgrad_ref.at[source], w_send.at[d - 1], w_recv.at[d - 1], partner).wait_recv()
    for copy in copies:
        copy.wait_send()
    for q in range(PIECES):
        pair(0, 0, q, chip).wait_send()
        for side, sign, hop in order:
            @pl.when(inside(chip + sign * hop, chips))
            def _():
                pair(side, hop, q, chip + sign * hop).wait_send()
                lane(side, hop, q, sign).wait_send()


def scatter_step(part, term, tiles, n_row, n_col):
    _, width, side = part.shape
    _, depth, hidden = term.shape
    chips = n_row // 2
    vmem = pl.BlockSpec(memory_space=pltpu.VMEM)
    dma = pltpu.SemaphoreType.DMA
    return pl.pallas_call(
        functools.partial(scatter_kernel, n_row, n_col),
        out_shape=(
            jax.ShapeDtypeStruct((width, tiles * side), BF16),
            jax.ShapeDtypeStruct((n_row, depth, hidden), F32),
        ),
        in_specs=[vmem, vmem],
        out_specs=(vmem, vmem),
        scratch_shapes=[
            pltpu.VMEM((2, chips, tiles, width, side), F32),
            pltpu.VMEM((2, chips - 1, tiles, width, side), BF16),
            pltpu.VMEM((2, chips - 1, tiles, width, side), BF16),
            pltpu.VMEM((tiles, width, side), F32),
            pltpu.VMEM((n_row - 1, depth, hidden), F32),
            pltpu.VMEM((n_col, depth, hidden), F32),
            pltpu.VMEM((depth, hidden), F32),
            dma((2, chips, PIECES)),
            dma((2, chips, PIECES)),
            dma((2, chips - 1, PIECES)),
            dma((2, chips - 1, PIECES)),
            dma((n_row - 1,)),
            dma((n_row - 1,)),
            dma((n_col - 1,)),
            dma((n_col - 1,)),
            dma((n_row - 1,)),
            dma((n_row - 1,)),
        ],
        compiler_params=pltpu.CompilerParams(
            collective_id=2, has_side_effects=True, vmem_limit_bytes=VMEM_LIMIT
        ),
        name="scatter_step",
    )(part, term)


def on_device(n_row, n_col, features, weight, cotangent, tile_values, tile_rows, tile_cols, tile_counts):
    own_rows, width = features.shape
    tiles = own_rows // 128
    sources, values, turned = gather_features(features.T, tile_values[0, 0], n_row)
    sources = sources.reshape(n_row * tiles, width, 128)
    part = tile_pass(turned, tile_rows, tile_cols, tile_counts, sources, n_col * tiles)
    activations, grads, term = node_step(
        part.reshape(n_col, tiles, width, 128), weight, cotangent, n_row, n_col
    )
    grads = grads.reshape(n_col * tiles, width, 128)
    grad_part, activations = tile_pass(
        values, tile_rows, tile_cols, tile_counts, grads, n_row * tiles, activations
    )
    out, weight_grad = scatter_step(grad_part, term, tiles, n_row, n_col)
    return activations, out.T, weight_grad.reshape(weight.shape)


def solution(mesh):
    in_specs = (
        P(("col", "row"), None),
        P(),
        P(("row", "col"), None),
        P("row", "col", None, None, None),
        P("row", "col", None),
        P("row", "col", None),
        P("row", "col"),
    )
    out_specs = (P(("row", "col"), None), P(("col", "row"), None), P())
    return jax.shard_map(
        functools.partial(on_device, mesh.shape["row"], mesh.shape["col"]),
        mesh=mesh,
        in_specs=in_specs,
        out_specs=out_specs,
        check_vma=False,
    )
```
